128 devices in a mesh: row: 16 (over z, x_lo, core), col: 8 (over x_hi, y).
Axes of the slice: x: 4 (x_hi: 2, x_lo: 2; x = x_hi * 2 + x_lo), y: 4, z: 4, core: 2. Of those that a mesh axis runs over, the one named last changes fastest.
Arguments:
- tile_values: bfloat16 [32768, 128, 128], P(('row', 'col')), may hold values from -0.09375 to 0.09375
- slot_codes: int32 [32768], P(('row', 'col')), may hold values from -1 to 511, as said below
- right_start: float32 [32768, 256], P(('row', 'col')), may hold values from -6 to 6
- left_start: float32 [32768, 256], P(('row', 'col')), may hold values from -6 to 6
- node_diagonal: float32 [32768], P(('row', 'col')), may hold values from 1 to 3
- row_scale: float32 [32768], P(('row', 'col')), may hold values from 0.2 to 15
Outputs:
- right_block: float32 [32768, 256], P(('row', 'col'))
- left_block: float32 [32768, 256], P(('row', 'col'))
- projections: float32 [2, 256, 256], replicated
The draws below stay inside these ranges and needn't reach their ends.
Inputs may be any that keep to these rules, and one draw needn't show every extreme that they name: `slot_codes`: slot (s, p, c) carries a tile that device s extracted for owner p; its code is -1 (empty) or a position a 32 + b in p's block grid of 16 x 2 * 16 places. The codes of one owner's live slots over all sources are distinct, so an owner receives at most 128 live tiles, and some owner receives exactly 128. A source fills at most 2 slots for one owner, and some source fills all 2.
All inputs are finite; a program needn't handle non-finite values.
Results may differ from the reference program's by a relative error of at most 0.002.
Values may be sent and summed in bfloat16 or wider, within the bound.
A program may use at most 128 MiB of HBM per device.

```python
import math
import jax
import jax.numpy as jnp
from jax import lax

TILE = 128
PORTS = 256
CAP = 2
ITERS = 2
OWNERS = 128
ORDER = 32768
N_ROW = 16
N_COL = 8


def permute_one(sub_key):
    return jax.random.permutation(sub_key, N_ROW * N_COL)


def permute_places(sub_key):
    return jax.random.permutation(sub_key, 4 * N_ROW * N_COL)


def draw_slot_codes(key, part):
    owners = N_ROW * N_COL
    key_busy = jax.random.fold_in(key, 11)
    key_forced = jax.random.fold_in(key, 12)
    key_light = jax.random.fold_in(key, 13)
    key_order = jax.random.fold_in(key, 14)
    key_place = jax.random.fold_in(key, 15)
    busy = jax.random.randint(key_busy, (owners,), 0, 8) == 0
    forced = jax.random.randint(key_forced, (), 0, owners)
    busy = jnp.logical_or(busy, jnp.arange(owners) == forced)
    light = jax.random.randint(key_light, (owners, owners), 0, 2)
    source_order = jax.vmap(permute_one)(jax.random.split(key_order, owners))
    source_rank = jnp.argsort(source_order, axis=1)
    heavy = jnp.where(source_rank < owners // 2, CAP, 0)
    counts = jnp.where(busy[:, None], heavy, light).astype(jnp.int32)
    starts = jnp.cumsum(counts, axis=1) - counts
    places = jax.vmap(permute_places)(jax.random.split(key_place, owners))
    slot_ids = jnp.arange(CAP, dtype=jnp.int32)
    index = starts[:, :, None] + slot_ids[None, None, :]
    live = slot_ids[None, None, :] < counts[:, :, None]
    safe_index = jnp.where(live, index, 0)
    picked = jnp.take_along_axis(places, safe_index.reshape(owners, owners * CAP), axis=1)
    codes = jnp.where(live, picked.reshape(owners, owners, CAP), -1)
    return jnp.transpose(codes, (1, 0, 2)).reshape(owners * owners * CAP).astype(jnp.int32)


def draw_row_scale(key, part):
    position = jnp.arange(ORDER).astype(jnp.float32)
    trend = jnp.exp(math.log(3.0) * position / ORDER)
    lower, upper = (math.log(0.3), math.log(3.0))
    spread = jax.random.uniform(key, (ORDER,), jnp.float32, lower, upper)
    return (jnp.exp(spread) * trend).astype(jnp.float32)


def block_levels(stream_key, shape, shards, low, largest):
    def one(dim, parts):
        steps = jax.random.uniform(jax.random.fold_in(jax.random.fold_in(stream_key, 6), dim), (parts,), jnp.float32, low / len(shards), largest / len(shards))
        return jnp.repeat(jnp.exp(steps), shape[dim] // parts).reshape((-1,) + (1,) * (len(shape) - dim - 1))

    factor_of = one(*shards[0])
    for cut in shards[1:]:
        factor_of = factor_of * one(*cut)
    return factor_of


def bell_draw(key, extent, width, bound, cuts=(), kind=jnp.bfloat16):
    gain = block_levels(key, extent, cuts, -0.22, 0.18) if cuts else 1.0
    array = jax.random.normal(key, extent, jnp.float32) * width * gain
    return jnp.minimum(jnp.maximum(array, -bound), bound).astype(kind)


def setup_inputs(seed: int = 0) -> dict:
    streams_of = jax.random.split(jax.random.key(seed), 7)
    return {
        "tile_values": bell_draw(streams_of[0], (OWNERS * OWNERS * CAP, TILE, TILE), (TILE * OWNERS // 4) ** -0.5, 0.09375, ((0, 128),)),
        "slot_codes": draw_slot_codes(jax.random.fold_in(streams_of[6], 71), 0),
        "right_start": bell_draw(streams_of[2], (ORDER, PORTS), 1.0, 6.0, ((0, 128),), jnp.float32),
        "left_start": bell_draw(streams_of[3], (ORDER, PORTS), 0.7, 6.0, ((0, 128),), jnp.float32),
        "node_diagonal": jnp.clip(1.0 + 2.0 * jax.random.uniform(streams_of[4], (ORDER,), jnp.float32) ** block_levels(streams_of[4], (ORDER,), ((0, 128),), -0.2, 0.2), 1.0, 3.0),
        "row_scale": draw_row_scale(jax.random.fold_in(streams_of[6], 71), 0),
    }


epsilon = 1e-06

def region_matrix(stacked_tiles, stacked_codes, owner_id, owners):
    places = 4 * owners
    slot_tiles = stacked_tiles[:, owner_id].reshape(owners * CAP, TILE, TILE)
    slot_keys = stacked_codes[:, owner_id].reshape(owners * CAP)
    safe_keys = jnp.where(slot_keys >= 0, slot_keys, places).astype(jnp.int32)
    region = jnp.zeros((places, TILE, TILE), jnp.float32)
    region = region.at[safe_keys].set(slot_tiles.astype(jnp.float32), mode='drop')
    region = region.reshape(2 * N_COL, 2 * N_ROW, TILE, TILE).transpose(0, 2, 1, 3)
    return region.reshape(2 * N_COL * TILE, 2 * N_ROW * TILE)

def apply_tiles(stacked_tiles, stacked_codes, right_bf, left_bf):
    owners = N_ROW * N_COL
    right_four = right_bf.reshape(N_ROW, N_COL, 2 * TILE, PORTS)
    left_four = left_bf.reshape(N_ROW, N_COL, 2 * TILE, PORTS)

    def accumulate(carry, owner_id):
        right_full, left_full = carry
        row_index = owner_id // N_COL
        col_index = owner_id % N_COL
        matrix = region_matrix(stacked_tiles, stacked_codes, owner_id, owners)
        right_cols = right_four[:, col_index].reshape(2 * N_ROW * TILE, PORTS).astype(jnp.float32)
        right_part = jnp.dot(matrix, right_cols, precision=lax.Precision.HIGHEST)
        right_full = right_full.at[row_index].add(right_part.reshape(N_COL, 2 * TILE, PORTS))
        left_rows = left_four[row_index].reshape(2 * N_COL * TILE, PORTS).astype(jnp.float32)
        left_part = jnp.dot(matrix.T, left_rows, precision=lax.Precision.HIGHEST)
        left_full = left_full.at[:, col_index].add(left_part.reshape(N_ROW, 2 * TILE, PORTS))
        return ((right_full, left_full), None)
    start = jnp.zeros((N_ROW, N_COL, 2 * TILE, PORTS), jnp.float32)
    (right_full, left_full), _ = lax.scan(accumulate, (start, start), jnp.arange(owners, dtype=jnp.int32))
    return (right_full.reshape(ORDER, PORTS), left_full.reshape(ORDER, PORTS))

def reference(tile_values, slot_codes, right_start, left_start, node_diagonal, row_scale):
    owners = N_ROW * N_COL
    stacked_tiles = tile_values.reshape(owners, owners, CAP, TILE, TILE)
    stacked_codes = slot_codes.reshape(owners, owners, CAP)
    scale_col = row_scale[:, None]
    diag_col = node_diagonal[:, None]
    right_vec = right_start
    left_vec = right_start + left_start
    stored = []
    for turn in range(ITERS):
        right_bf = right_vec.astype(jnp.bfloat16)
        scaled_left = scale_col * left_vec
        left_bf = scaled_left.astype(jnp.bfloat16)
        right_prod, left_prod = apply_tiles(stacked_tiles, stacked_codes, right_bf, left_bf)
        right_new = scale_col * (right_prod + diag_col * right_vec)
        left_new = left_prod + diag_col * scaled_left
        project = jnp.dot(left_vec.T, right_new, precision=lax.Precision.HIGHEST) / ORDER
        right_rest = right_new - jnp.dot(right_vec, project, precision=lax.Precision.HIGHEST)
        left_rest = left_new - jnp.dot(left_vec, project.T, precision=lax.Precision.HIGHEST)
        right_norm = jnp.sqrt(lax.optimization_barrier(jnp.sum(right_rest * right_rest, axis=0)) / ORDER + epsilon)
        left_norm = jnp.sqrt(lax.optimization_barrier(jnp.sum(left_rest * left_rest, axis=0)) / ORDER + epsilon)
        right_vec = right_rest / right_norm[None, :]
        left_vec = left_rest / left_norm[None, :]
        stored.append(project)
    return (right_vec, left_vec, jnp.stack(stored))
```

```python
import functools

import jax
import jax.numpy as jnp
from jax import lax
from jax.experimental import pallas as pl
from jax.experimental.pallas import tpu as pltpu
from jax.sharding import PartitionSpec as P

ITERS = 2
epsilon = 1e-06
MESH = pl.DeviceIdType.MESH
F32 = jnp.float32
BF16 = jnp.bfloat16
HIGHEST = lax.Precision.HIGHEST


def span(index, size):
    return pl.ds(pl.multiple_of(index * size, size), size)


def krylov_kernel(
    nr, nc, order,
    slots_ref, tiles_hbm, right_ref, left_ref, diag_col, diag_row, scale_col, scale_row,
    v_out, w_out, h_out,
    tiles, ta, vg, wg, wt, r_new, lt_new,
    r_send, r_recv, sib_send, sib_recv, l_send, l_recv,
    h_loc, h_part, h_from_row, h_from_col, h_full,
    n_loc, n_part, n_from_row, n_from_col,
    tile_sem, v_ss, v_rs, f_ss, f_rs, w_ss, w_rs, r_ss, r_rs, s_ss, s_rs, l_ss, l_rs,
    h1_ss, h1_rs, h2_ss, h2_rs, h3_ss, h3_rs, n1_ss, n1_rs, n2_ss, n2_rs,
):
    row, col = lax.axis_index("row"), lax.axis_index("col")
    nq = nr // 2
    chip, core = row // 2, row % 2
    sibling = chip * 2 + (1 - core)
    tile = tiles.shape[1]
    block = 2 * tile
    slot_total = tiles_hbm.shape[0]
    h_rows = h_loc.shape[0] // nr

    def row_at(d):
        return lax.rem(row + d, nr)

    def col_at(d):
        return lax.rem(col + d, nc)

    def chip_at(d):
        return lax.rem(chip + d, nq) * 2 + core

    def each(low, high, body):
        def step(i, carry):
            body(i)
            return carry

        lax.fori_loop(low, high, step, 0)

    def remote(src, dst, send, recv, r, c):
        return pltpu.make_async_remote_copy(
            src_ref=src, dst_ref=dst, send_sem=send, recv_sem=recv,
            device_id=(r, c), device_id_type=MESH,
        )

    def v_copy(d, r):
        at = vg.at[span(r, block)]
        return remote(at, at, v_ss.at[d - 1], v_rs.at[d - 1], chip_at(d), col)

    def f_copy(e, r):
        at = vg.at[span(r, block)]
        return remote(at, at, f_ss.at[e], f_rs.at[e], sibling, col)

    def w_copy(d, c):
        return remote(wg.at[c], wg.at[c], w_ss.at[d - 1], w_rs.at[d - 1], row, col_at(d))

    def r_copy(d):
        return remote(r_send.at[d - 1], r_recv.at[d - 1], r_ss.at[d - 1], r_rs.at[d - 1], row, col_at(d))

    def s_copy(e):
        return remote(sib_send.at[e], sib_recv.at[e], s_ss.at[e], s_rs.at[e], sibling, col)

    def l_copy(d):
        return remote(l_send.at[d - 1], l_recv.at[d - 1], l_ss.at[d - 1], l_rs.at[d - 1], chip_at(d), col)

    def h1_copy(d, src, slot):
        return remote(
            h_loc.at[span(src, h_rows)], h_from_row.at[slot], h1_ss.at[d - 1], h1_rs.at[d - 1], row_at(d), col
        )

    def h2_copy(d, slot):
        return remote(h_part, h_from_col.at[slot], h2_ss.at[d - 1], h2_rs.at[d - 1], row, col_at(d))

    def h3_copy(d, slot):
        at = h_full.at[span(slot, h_rows)]
        return remote(at, at, h3_ss.at[d - 1], h3_rs.at[d - 1], row_at(d), col)

    def n1_copy(d, slot):
        return remote(n_loc, n_from_row.at[slot], n1_ss.at[d - 1], n1_rs.at[d - 1], row_at(d), col)

    def n2_copy(d, slot):
        return remote(n_part, n_from_col.at[slot], n2_ss.at[d - 1], n2_rs.at[d - 1], row, col_at(d))

    def row_behind(d):
        return lax.rem(row - d + nr, nr)

    def col_behind(d):
        return lax.rem(col - d + nc, nc)

    def chip_behind(d):
        return lax.rem(chip - d + nq, nq) * 2 + core

    load = pltpu.make_async_copy(tiles_hbm, tiles.at[pl.ds(0, slot_total)], tile_sem)
    load.start()

    barrier = pltpu.get_barrier_semaphore()
    each(1, nr, lambda d: pl.semaphore_signal(barrier, inc=1, device_id=(row_at(d), col), device_id_type=MESH))
    each(1, nc, lambda d: pl.semaphore_signal(barrier, inc=1, device_id=(row, col_at(d)), device_id_type=MESH))
    start_right = right_ref[...]
    v_out[...] = start_right
    wt[...] = jnp.transpose(start_right + left_ref[...])
    pl.semaphore_wait(barrier, nr + nc - 2)

    def assemble():
        load.wait()
        tiles[slot_total] = jnp.zeros((tile, tile), BF16)

        def one_row(a):
            for b in range(2 * nr):
                ta[span(a, tile), b * tile : (b + 1) * tile] = tiles[slots_ref[a * 2 * nr + b]]

        each(0, 2 * nc, one_row)

    def iteration(turn):
        vg[span(row, block)] = v_out[...].astype(BF16)
        each(1, nq, lambda d: v_copy(d, row).start())
        f_copy(0, row).start()
        scaled = scale_row[...] * wt[...]
        wg[col] = scaled.astype(BF16)
        each(1, nc, lambda d: w_copy(d, col).start())

        @pl.when(turn == 0)
        def _():
            assemble()

        def forward(d):
            v_copy(d, chip_behind(d)).wait_recv()
            f_copy(d, chip_behind(d)).start()

        each(1, nq, forward)

        def from_sibling(e):
            at = lax.rem(chip - e + nq, nq) * 2 + (1 - core)
            f_copy(e, at).wait_recv()

        each(0, nq, from_sibling)

        def right_part(c):
            return jnp.dot(ta[span(c, block)], vg[...], preferred_element_type=F32)

        def right_step(d):
            r_send[d - 1] = right_part(col_at(d)).astype(BF16)
            r_copy(d).start()

        each(1, nc, right_step)
        r_new[...] = right_part(col) + diag_col[...] * v_out[...]

        def v_sent(d):
            v_copy(d, row).wait_send()
            f_copy(d, row).wait_send()

        f_copy(0, row).wait_send()
        each(1, nq, v_sent)

        def right_sum(d):
            r_copy(d).wait_recv()
            r_new[...] += r_recv[d - 1].astype(F32)

        each(1, nc, right_sum)
        r_new[...] = scale_col[...] * r_new[...]

        h_loc[...] = jnp.dot(wt[...], r_new[...], precision=HIGHEST, preferred_element_type=F32)
        each(1, nr, lambda d: h1_copy(d, row_at(d), row).start())
        h_from_row[row] = h_loc[span(row, h_rows)]

        each(1, nc, lambda d: w_copy(d, col_behind(d)).wait_recv())

        def left_part(r):
            rows = jnp.concatenate([wg[c] for c in range(nc)], axis=1)
            return jnp.dot(rows, ta[:, span(r, block)], preferred_element_type=F32)

        def left_other(e):
            sib_send[e] = left_part(lax.rem(chip + e, nq) * 2 + (1 - core))
            s_copy(e).start()

        each(0, nq, left_other)

        each(1, nr, lambda d: h1_copy(d, row_at(d), row_behind(d)).wait_recv())
        part = h_from_row[0]
        for i in range(1, nr):
            part += h_from_row[i]
        h_part[...] = part
        each(1, nc, lambda d: h2_copy(d, col).start())
        h_from_col[col] = part

        def left_own(e):
            s_copy(e).wait_recv()
            l_send[e - 1] = (left_part(chip_at(e)) + sib_recv[e]).astype(BF16)
            l_copy(e).start()

        each(1, nq // 2, left_own)

        each(1, nc, lambda d: h2_copy(d, col_behind(d)).wait_recv())
        total = h_from_col[0]
        for i in range(1, nc):
            total += h_from_col[i]
        h_full[span(row, h_rows)] = total * (1.0 / order)
        each(1, nr, lambda d: h3_copy(d, row).start())

        each(nq // 2, nq, left_own)
        s_copy(0).wait_recv()
        scaled_again = scale_row[...] * wt[...]
        lt_new[...] = left_part(row) + sib_recv[0] + diag_row[...] * scaled_again

        each(1, nr, lambda d: h3_copy(d, row_behind(d)).wait_recv())
        project = h_full[...]
        h_out[turn] = project
        rest = r_new[...] - jnp.dot(v_out[...], project, precision=HIGHEST, preferred_element_type=F32)
        r_new[...] = rest
        n_loc[0:1] = jnp.sum(rest * rest, axis=0, keepdims=True)
        lt_new[...] -= jnp.dot(project, wt[...], precision=HIGHEST, preferred_element_type=F32)

        def left_sum(d):
            l_copy(d).wait_recv()
            lt_new[...] += l_recv[d - 1].astype(F32)

        each(1, nq, left_sum)
        left_rest = lt_new[...]
        n_loc[1:2] = jnp.sum(jnp.transpose(left_rest * left_rest), axis=0, keepdims=True)

        each(1, nc, lambda d: w_copy(d, col).wait_send())
        each(1, nc, lambda d: r_copy(d).wait_send())
        each(0, nq, lambda e: s_copy(e).wait_send())
        each(1, nq, lambda d: l_copy(d).wait_send())
        each(1, nr, lambda d: h1_copy(d, row_at(d), row).wait_send())
        each(1, nc, lambda d: h2_copy(d, col).wait_send())
        each(1, nr, lambda d: h3_copy(d, row).wait_send())

        each(1, nr, lambda d: n1_copy(d, row).start())
        n_from_row[row] = n_loc[...]
        each(1, nr, lambda d: n1_copy(d, row_behind(d)).wait_recv())
        sums = n_from_row[0]
        for i in range(1, nr):
            sums += n_from_row[i]
        n_part[...] = sums
        each(1, nc, lambda d: n2_copy(d, col).start())
        n_from_col[col] = sums
        each(1, nr, lambda d: n1_copy(d, row).wait_send())
        each(1, nc, lambda d: n2_copy(d, col_behind(d)).wait_recv())
        sums = n_from_col[0]
        for i in range(1, nc):
            sums += n_from_col[i]
        each(1, nc, lambda d: n2_copy(d, col).wait_send())
        norms = jnp.sqrt(sums * (1.0 / order) + epsilon)
        v_out[...] = r_new[...] / norms[0:1]
        ports = lt_new.shape[0]
        wt[...] = lt_new[...] / jnp.transpose(jnp.broadcast_to(norms[1:2], (lt_new.shape[1], ports)))

    n_loc[...] = jnp.zeros_like(n_loc)
    each(0, ITERS, iteration)
    w_out[...] = jnp.transpose(wt[...])


def local(tile_values, slot_codes, right_start, left_start, node_diagonal, row_scale):
    nr, nc = lax.axis_size("row"), lax.axis_size("col")
    slot_total, tile = tile_values.shape[:2]
    rows, ports = right_start.shape
    order = rows * nr * nc
    nq = nr // 2
    got_tiles = lax.all_to_all(tile_values, ("row", "col"), split_axis=0, concat_axis=0, tiled=True)
    got_codes = lax.all_to_all(slot_codes, ("row", "col"), split_axis=0, concat_axis=0, tiled=True)
    places = 4 * nr * nc
    hit = got_codes[None, :] == jnp.arange(places, dtype=jnp.int32)[:, None]
    slots = jnp.max(jnp.where(hit, jnp.arange(slot_total, dtype=jnp.int32)[None, :], -1), axis=1)
    slots = jnp.where(slots < 0, slot_total, slots)
    vmem = pl.BlockSpec(memory_space=pltpu.VMEM)
    sem = pltpu.SemaphoreType.DMA
    counts = (nq - 1, nq, nc - 1, nc - 1, nq, nq - 1, nr - 1, nc - 1, nr - 1, nr - 1, nc - 1)
    h_rows = ports // nr
    return pl.pallas_call(
        functools.partial(krylov_kernel, nr, nc, order),
        out_shape=(
            jax.ShapeDtypeStruct((rows, ports), F32),
            jax.ShapeDtypeStruct((rows, ports), F32),
            jax.ShapeDtypeStruct((ITERS, ports, ports), F32),
        ),
        in_specs=[
            pl.BlockSpec(memory_space=pltpu.SMEM),
            pl.BlockSpec(memory_space=pl.ANY),
            vmem, vmem, vmem, vmem, vmem, vmem,
        ],
        out_specs=(vmem, vmem, vmem),
        scratch_shapes=[
            pltpu.VMEM((slot_total + 1, tile, tile), BF16),
            pltpu.VMEM((2 * nc * tile, 2 * nr * tile), BF16),
            pltpu.VMEM((nr * rows, ports), BF16),
            pltpu.VMEM((nc, ports, rows), BF16),
            pltpu.VMEM((ports, rows), F32),
            pltpu.VMEM((rows, ports), F32),
            pltpu.VMEM((ports, rows), F32),
            pltpu.VMEM((nc - 1, rows, ports), BF16),
            pltpu.VMEM((nc - 1, rows, ports), BF16),
            pltpu.VMEM((nq, ports, rows), F32),
            pltpu.VMEM((nq, ports, rows), F32),
            pltpu.VMEM((nq - 1, ports, rows), BF16),
            pltpu.VMEM((nq - 1, ports, rows), BF16),
            pltpu.VMEM((ports, ports), F32),
            pltpu.VMEM((h_rows, ports), F32),
            pltpu.VMEM((nr, h_rows, ports), F32),
            pltpu.VMEM((nc, h_rows, ports), F32),
            pltpu.VMEM((ports, ports), F32),
            pltpu.VMEM((8, ports), F32),
            pltpu.VMEM((8, ports), F32),
            pltpu.VMEM((nr, 8, ports), F32),
            pltpu.VMEM((nc, 8, ports), F32),
            sem,
        ]
        + [sem((n,)) for n in counts for _ in range(2)],
        compiler_params=pltpu.CompilerParams(
            collective_id=0, has_side_effects=True, vmem_limit_bytes=58 * 2**20
        ),
        name="krylov",
    )(
        slots, got_tiles, right_start, left_start,
        node_diagonal[:, None], node_diagonal[None, :], row_scale[:, None], row_scale[None, :],
    )


def solution(mesh):
    return jax.shard_map(
        local,
        mesh=mesh,
        in_specs=(
            P(("row", "col"), None, None),
            P(("row", "col")),
            P(("row", "col"), None),
            P(("row", "col"), None),
            P(("row", "col")),
            P(("row", "col")),
        ),
        out_specs=(P(("row", "col"), None), P(("row", "col"), None), P()),
        check_vma=False,
    )
```

```python
import functools

import jax
import jax.numpy as jnp
from jax import lax
from jax.experimental import pallas as pl
from jax.experimental.pallas import tpu as pltpu
from jax.sharding import PartitionSpec as P

ITERS = 2
epsilon = 1e-06
MESH = pl.DeviceIdType.MESH
F32 = jnp.float32
BF16 = jnp.bfloat16
HIGHEST = lax.Precision.HIGHEST


def span(index, size):
    return pl.ds(pl.multiple_of(index * size, size), size)


def each(low, high, body):
    def step(i, carry):
        body(i)
        return carry

    lax.fori_loop(low, high, step, 0)


def remote(src, dst, send, recv, to):
    return pltpu.make_async_remote_copy(
        src_ref=src, dst_ref=dst, send_sem=send, recv_sem=recv, device_id=to, device_id_type=MESH
    )


class Place:
    def __init__(self, nr, nc):
        self.nr, self.nc, self.nz, self.ny = nr, nc, nr // 4, nc // 2
        self.row, self.col = lax.axis_index("row"), lax.axis_index("col")
        self.z, self.xl, self.core = self.row // 4, (self.row // 2) % 2, self.row % 2
        self.xh, self.y = self.col // self.ny, self.col % self.ny

    def row_at(self, d):
        return lax.rem(self.row + d + self.nr, self.nr)

    def col_at(self, d):
        return lax.rem(self.col + d + self.nc, self.nc)

    def z_at(self, d):
        return lax.rem(self.z + d + self.nz, self.nz)

    def y_at(self, d):
        return lax.rem(self.y + d + self.ny, self.ny)

    def row_of(self, z, xl, core):
        return z * 4 + xl * 2 + core

    def col_of(self, xh, y):
        return xh * self.ny + y

    def greet(self):
        barrier = pltpu.get_barrier_semaphore()
        each(1, self.nr, lambda d: pl.semaphore_signal(
            barrier, inc=1, device_id=(self.row_at(d), self.col), device_id_type=MESH))
        each(1, self.nc, lambda d: pl.semaphore_signal(
            barrier, inc=1, device_id=(self.row, self.col_at(d)), device_id_type=MESH))
        return lambda: pl.semaphore_wait(barrier, self.nr + self.nc - 2)


class RightGather:
    def __init__(self, me, vg, block, sems):
        self.me, self.vg, self.block = me, vg, block
        self.x_ss, self.x_rs, self.z_ss, self.z_rs, self.f_ss, self.f_rs = sems

    def slot(self, r):
        return self.vg.at[span(r, self.block)]

    def x_copy(self, r):
        me = self.me
        return remote(self.slot(r), self.slot(r), self.x_ss, self.x_rs, (me.row_of(me.z, 1 - me.xl, me.core), me.col))

    def z_copy(self, second, d, r):
        me = self.me
        i = second * (me.nz - 1) + d - 1
        to = (me.row_of(me.z_at(d), me.xl, me.core), me.col)
        return remote(self.slot(r), self.slot(r), self.z_ss.at[i], self.z_rs.at[i], to)

    def f_copy(self, second, d, r):
        me = self.me
        i = second * me.nz + d
        to = (me.row_of(me.z, me.xl, 1 - me.core), me.col)
        return remote(self.slot(r), self.slot(r), self.f_ss.at[i], self.f_rs.at[i], to)

    def from_z(self, second, d, other=0):
        me = self.me
        xl = 1 - me.xl if second else me.xl
        core = 1 - me.core if other else me.core
        return me.row_of(me.z_at(-d), xl, core)

    def start(self):
        me = self.me
        self.x_copy(me.row).start()
        each(1, me.nz, lambda d: self.z_copy(0, d, me.row).start())
        self.f_copy(0, 0, me.row).start()

    def pass_x(self):
        r = self.from_z(1, 0)
        self.x_copy(r).wait_recv()
        each(1, self.me.nz, lambda d: self.z_copy(1, d, r).start())
        self.f_copy(1, 0, r).start()

    def pass_z(self):
        for second in range(2):
            def one(d, second=second):
                r = self.from_z(second, d)
                self.z_copy(second, d, r).wait_recv()
                self.f_copy(second, d, r).start()

            each(1, self.me.nz, one)

    def arrive(self):
        for second in range(2):
            each(0, self.me.nz, lambda d, second=second: self.f_copy(
                second, d, self.from_z(second, d, 1)).wait_recv())

    def sent(self):
        me = self.me
        self.x_copy(me.row).wait_send()
        for second in range(2):
            each(1, me.nz, lambda d, second=second: self.z_copy(second, d, me.row).wait_send())
            each(0, me.nz, lambda d, second=second: self.f_copy(second, d, me.row).wait_send())


class LeftGather:
    def __init__(self, me, wg, sems):
        self.me, self.wg = me, wg
        self.x_ss, self.x_rs, self.y_ss, self.y_rs = sems

    def x_copy(self, c):
        me = self.me
        return remote(self.wg.at[c], self.wg.at[c], self.x_ss, self.x_rs, (me.row, me.col_of(1 - me.xh, me.y)))

    def y_copy(self, second, d, c):
        me = self.me
        i = second * (me.ny - 1) + d - 1
        to = (me.row, me.col_of(me.xh, me.y_at(d)))
        return remote(self.wg.at[c], self.wg.at[c], self.y_ss.at[i], self.y_rs.at[i], to)

    def start(self):
        me = self.me
        self.x_copy(me.col).start()
        each(1, me.ny, lambda d: self.y_copy(0, d, me.col).start())

    def pass_x(self):
        me = self.me
        c = me.col_of(1 - me.xh, me.y)
        self.x_copy(c).wait_recv()
        each(1, me.ny, lambda d: self.y_copy(1, d, c).start())

    def arrive(self):
        me = self.me
        for second in range(2):
            xh = 1 - me.xh if second else me.xh
            each(1, me.ny, lambda d, second=second, xh=xh: self.y_copy(
                second, d, me.col_of(xh, me.y_at(-d))).wait_recv())

    def sent(self):
        me = self.me
        self.x_copy(me.col).wait_send()
        for second in range(2):
            each(1, me.ny, lambda d, second=second: self.y_copy(second, d, me.col).wait_send())


class Exchange:
    def __init__(self, me, along_row, src, slots, ss, rs, pick=None):
        self.me, self.along_row, self.src, self.slots, self.ss, self.rs = me, along_row, src, slots, ss, rs
        self.pick = pick or (lambda i: src)
        self.size = me.nr if along_row else me.nc
        self.mine = me.row if along_row else me.col

    def at(self, d):
        return self.me.row_at(d) if self.along_row else self.me.col_at(d)

    def copy(self, d, slot):
        me = self.me
        to = (self.at(d), me.col) if self.along_row else (me.row, self.at(d))
        return remote(self.pick(self.at(d)), self.slots.at[slot], self.ss.at[d - 1], self.rs.at[d - 1], to)

    def start(self):
        each(1, self.size, lambda d: self.copy(d, self.mine).start())

    def total(self):
        each(1, self.size, lambda d: self.copy(d, self.at(-d)).wait_recv())
        total = self.slots[0]
        for i in range(1, self.size):
            total += self.slots[i]
        return total

    def sent(self):
        each(1, self.size, lambda d: self.copy(d, self.mine).wait_send())


def gather_kernel(nr, nc, codes, right, left, scale_row, vg, wg, got, got_row, *sems):
    me = Place(nr, nc)
    hold = me.greet()
    block = right.shape[0]
    v = RightGather(me, vg, block, sems[:6])
    w = LeftGather(me, wg, sems[6:10])
    c1_ss, c1_rs, c2_ss, c2_rs = sems[10:14]
    start_right = right[...]
    vg[span(me.row, block)] = start_right.astype(BF16)
    wg[me.col] = (scale_row[...] * jnp.transpose(start_right + left[...])).astype(BF16)
    got_row[me.row] = codes[me.row]

    def c1_copy(d, slot):
        return remote(codes.at[me.row_at(d)], got_row.at[slot], c1_ss.at[d - 1], c1_rs.at[d - 1],
                      (me.row_at(d), me.col))

    def c2_copy(d, slot):
        return remote(got_row, got.at[slot], c2_ss.at[d - 1], c2_rs.at[d - 1], (me.row, me.col_at(d)))

    hold()
    each(1, nr, lambda d: c1_copy(d, me.row).start())
    each(1, nr, lambda d: c1_copy(d, me.row_at(-d)).wait_recv())
    each(1, nc, lambda d: c2_copy(d, me.col).start())
    v.start()
    w.start()
    got[me.col] = got_row[...]
    v.pass_x()
    w.pass_x()
    v.pass_z()
    each(1, nc, lambda d: c2_copy(d, me.col_at(-d)).wait_recv())
    w.arrive()
    v.arrive()
    v.sent()
    w.sent()
    each(1, nr, lambda d: c1_copy(d, me.row).wait_send())
    each(1, nc, lambda d: c2_copy(d, me.col).wait_send())


def krylov_kernel(
    nr, nc, order,
    slots_ref, tiles_hbm, vg_hbm, wg_hbm, right_ref, left_ref, diag_col, diag_row, scale_col, scale_row,
    r_new, lt_new, norm_out, h_out,
    tiles, ta, vg, wg, v_ref, wt,
    r_send, r_recv, sib_send, sib_recv, l_send, l_recv, l_keep, x_send, x_recv,
    h_loc, h_part, h_from_row, h_from_col, h_full,
    n_loc, n_part, n_from_row, n_from_col, m_loc, m_part, m_from_row, m_from_col,
    tile_sem, vg_sem, wg_sem, *sems,
):
    me = Place(nr, nc)
    row, col, nz = me.row, me.col, me.nz
    tile = tiles.shape[1]
    block = 2 * tile
    slot_total = tiles_hbm.shape[0]
    h_rows = h_loc.shape[0] // nr
    v = RightGather(me, vg, block, sems[:6])
    w = LeftGather(me, wg, sems[6:10])
    (r_ss, r_rs, s_ss, s_rs, l_ss, l_rs, x_ss, x_rs, h1_ss, h1_rs, h2_ss, h2_rs, h3_ss, h3_rs,
     n1_ss, n1_rs, n2_ss, n2_rs, m1_ss, m1_rs, m2_ss, m2_rs) = sems[10:]

    def r_copy(d):
        return remote(r_send.at[d - 1], r_recv.at[d - 1], r_ss.at[d - 1], r_rs.at[d - 1], (row, me.col_at(d)))

    def s_copy(e):
        to = (me.row_of(me.z, me.xl, 1 - me.core), col)
        return remote(sib_send.at[e], sib_recv.at[e], s_ss.at[e], s_rs.at[e], to)

    def l_copy(d):
        to = (me.row_of(me.z_at(d), me.xl, me.core), col)
        return remote(l_send.at[d - 1], l_recv.at[d - 1], l_ss.at[d - 1], l_rs.at[d - 1], to)

    def x_copy():
        return remote(x_send, x_recv, x_ss, x_rs, (me.row_of(me.z, 1 - me.xl, me.core), col))

    def h3_copy(d, slot):
        at = h_full.at[span(slot, h_rows)]
        return remote(at, at, h3_ss.at[d - 1], h3_rs.at[d - 1], (me.row_at(d), col))

    h1 = Exchange(me, True, h_loc, h_from_row, h1_ss, h1_rs, lambda i: h_loc.at[span(i, h_rows)])
    h2 = Exchange(me, False, h_part, h_from_col, h2_ss, h2_rs)
    n1 = Exchange(me, True, n_loc, n_from_row, n1_ss, n1_rs)
    n2 = Exchange(me, False, n_part, n_from_col, n2_ss, n2_rs)
    m1 = Exchange(me, True, m_loc, m_from_row, m1_ss, m1_rs)
    m2 = Exchange(me, False, m_part, m_from_col, m2_ss, m2_rs)

    load = pltpu.make_async_copy(tiles_hbm, tiles.at[pl.ds(0, slot_total)], tile_sem)
    load.start()
    load_vg = pltpu.make_async_copy(vg_hbm, vg, vg_sem)
    load_vg.start()
    load_wg = pltpu.make_async_copy(wg_hbm, wg, wg_sem)
    load_wg.start()
    hold = me.greet()
    wt[...] = jnp.transpose(right_ref[...] + left_ref[...])
    v_ref[...] = right_ref[...]
    n_loc[...] = jnp.zeros_like(n_loc)
    m_loc[...] = jnp.zeros_like(m_loc)
    tiles[slot_total] = jnp.zeros((tile, tile), BF16)
    load.wait()

    def one_row(a):
        for b in range(2 * nr):
            ta[span(a, tile), b * tile : (b + 1) * tile] = tiles[slots_ref[a * 2 * nr + b]]

    each(0, 2 * nc, one_row)
    load_vg.wait()
    load_wg.wait()
    hold()

    def right_part(c):
        return jnp.dot(ta[span(c, block)], vg[...], preferred_element_type=F32)

    def left_part(r):
        rows = jnp.concatenate([wg[c] for c in range(nc)], axis=1)
        return jnp.dot(rows, ta[:, span(r, block)], preferred_element_type=F32)

    def norm_of(total):
        return jnp.sqrt(total * (1.0 / order) + epsilon)

    for turn in range(ITERS):
        last = turn == ITERS - 1
        if turn:
            v.arrive()

        def right_step(d):
            r_send[d - 1] = right_part(me.col_at(d)).astype(BF16)
            r_copy(d).start()

        each(1, nc, right_step)
        r_new[...] = right_part(col) + diag_col[...] * v_ref[...]

        if turn:
            w.arrive()

        def left_other(e):
            sib_send[e] = left_part(me.row_of(me.z_at(e // 2), e % 2, 1 - me.core))
            s_copy(e).start()

        each(2, 2 * nz, left_other)
        each(0, 2, left_other)

        def left_own(e):
            s_copy(e).wait_recv()
            return left_part(me.row_of(me.z_at(e // 2), e % 2, me.core)) + sib_recv[e]

        def left_away(d):
            for i in range(2):
                l_send[d - 1, i] = left_own(2 * d + i).astype(BF16)
            l_copy(d).start()

        each(1, nz, left_away)

        def left_home(i):
            l_keep[i] = left_own(i)

        each(0, 2, left_home)

        def right_sum(d):
            r_copy(d).wait_recv()
            r_new[...] += r_recv[d - 1].astype(F32)

        each(1, nc, right_sum)
        r_new[...] = scale_col[...] * r_new[...]

        h_loc[...] = jnp.dot(wt[...], r_new[...], precision=HIGHEST, preferred_element_type=F32)
        h1.start()
        h_from_row[row] = h_loc[span(row, h_rows)]
        part = h1.total()
        h_part[...] = part
        h2.start()
        h_from_col[col] = part

        def left_sum(d):
            l_copy(d).wait_recv()
            for i in range(2):
                l_keep[i] += l_recv[d - 1, i].astype(F32)

        each(1, nz, left_sum)
        x_send[...] = l_keep[1 - me.xl]
        x_copy().start()

        h_full[span(row, h_rows)] = h2.total() * (1.0 / order)
        each(1, nr, lambda d: h3_copy(d, row).start())
        scaled = scale_row[...] * wt[...]
        lt_new[...] = l_keep[me.xl] + diag_row[...] * scaled
        each(1, nr, lambda d: h3_copy(d, me.row_at(-d)).wait_recv())

        project = h_full[...]
        rest = r_new[...] - jnp.dot(v_ref[...], project, precision=HIGHEST, preferred_element_type=F32)
        r_new[...] = rest
        n_loc[0:1] = jnp.sum(rest * rest, axis=0, keepdims=True)
        if not last:
            n1.start()
            n_from_row[row] = n_loc[...]

        h_out[turn] = h_full[...]
        lt_new[...] -= jnp.dot(h_full[...], wt[...], precision=HIGHEST, preferred_element_type=F32)
        x_copy().wait_recv()
        lt_new[...] += x_recv[...]
        left_rest = lt_new[...]
        left_norm = jnp.sum(jnp.transpose(left_rest * left_rest), axis=0, keepdims=True)
        if last:
            n_loc[1:2] = left_norm
            n1.start()
            n_from_row[row] = n_loc[...]
        else:
            m_loc[0:1] = left_norm
        n_part[...] = n1.total()
        n2.start()
        n_from_col[col] = n_part[...]

        if turn:
            v.sent()
            w.sent()
        each(1, nc, lambda d: r_copy(d).wait_send())
        each(0, 2 * nz, lambda e: s_copy(e).wait_send())
        each(1, nz, lambda d: l_copy(d).wait_send())
        x_copy().wait_send()
        h1.sent()
        h2.sent()
        each(1, nr, lambda d: h3_copy(d, row).wait_send())
        n1.sent()
        total = n2.total()
        n2.sent()
        if last:
            norm_out[...] = norm_of(total)
        else:
            v_new = r_new[...] / norm_of(total)[0:1]
            v_ref[...] = v_new
            vg[span(row, block)] = v_new.astype(BF16)
            v.start()
            m1.start()
            m_from_row[row] = m_loc[...]
            v.pass_x()
            m_part[...] = m1.total()
            m2.start()
            m_from_col[col] = m_part[...]
            m1.sent()
            norm = norm_of(m2.total())[0:1]
            m2.sent()
            size = lt_new.shape
            w_new = lt_new[...] / jnp.transpose(jnp.broadcast_to(norm, (size[1], size[0])))
            wt[...] = w_new
            wg[col] = (scale_row[...] * w_new).astype(BF16)
            w.start()
            v.pass_z()
            w.pass_x()


def finish_kernel(r_ref, lt_ref, norm_ref, h_ref, v_out, w_out, h_out):
    v_out[...] = r_ref[...] / norm_ref[0:1]
    w_out[...] = jnp.transpose(lt_ref[...]) / norm_ref[1:2]
    h_out[...] = h_ref[...]


def local(tile_values, slot_codes, right_start, left_start, node_diagonal, row_scale):
    nr, nc = lax.axis_size("row"), lax.axis_size("col")
    slot_total, tile = tile_values.shape[:2]
    rows, ports = right_start.shape
    order = rows * nr * nc
    nz, ny = nr // 4, nc // 2
    vmem = pl.BlockSpec(memory_space=pltpu.VMEM)
    any_space = pl.BlockSpec(memory_space=pl.ANY)
    sem = pltpu.SemaphoreType.DMA
    scale_row = row_scale[None, :]

    def pairs(*counts):
        return [sem((n,)) if n else sem for n in counts for _ in range(2)]

    gather_sems = pairs(0, 2 * (nz - 1), 2 * nz, 0, 2 * (ny - 1))

    got_tiles = lax.all_to_all(tile_values, ("row", "col"), split_axis=0, concat_axis=0, tiled=True)
    codes = jnp.pad(slot_codes.reshape(nr, 1, 2 * nc), ((0, 0), (0, 7), (0, 128 - 2 * nc)))
    vg, wg, got = pl.pallas_call(
        functools.partial(gather_kernel, nr, nc),
        out_shape=(
            jax.ShapeDtypeStruct((nr * rows, ports), BF16),
            jax.ShapeDtypeStruct((nc, ports, rows), BF16),
            jax.ShapeDtypeStruct((nc, nr, 8, 128), jnp.int32),
        ),
        in_specs=[vmem] * 4,
        out_specs=(vmem,) * 3,
        scratch_shapes=[pltpu.VMEM((nr, 8, 128), jnp.int32)] + gather_sems + pairs(nr - 1, nc - 1),
        compiler_params=pltpu.CompilerParams(
            collective_id=0, has_side_effects=True, vmem_limit_bytes=16 * 2**20
        ),
        cost_estimate=pl.CostEstimate(flops=10**10, bytes_accessed=10**7, transcendentals=0),
        name="gather",
    )(codes, right_start, left_start, scale_row)

    got = lax.dynamic_slice_in_dim(got[:, :, 0, :], 2 * lax.axis_index("col"), 2, axis=2)
    got_codes = jnp.transpose(got, (1, 0, 2)).reshape(slot_total)
    places = 4 * nr * nc
    hit = got_codes[None, :] == jnp.arange(places, dtype=jnp.int32)[:, None]
    slots = jnp.max(jnp.where(hit, jnp.arange(slot_total, dtype=jnp.int32)[None, :], -1), axis=1)
    slots = jnp.where(slots < 0, slot_total, slots)

    h_rows = ports // nr
    right_rest, left_rest, norms, projections = pl.pallas_call(
        functools.partial(krylov_kernel, nr, nc, order),
        out_shape=(
            jax.ShapeDtypeStruct((rows, ports), F32),
            jax.ShapeDtypeStruct((ports, rows), F32),
            jax.ShapeDtypeStruct((8, ports), F32),
            jax.ShapeDtypeStruct((ITERS, ports, ports), F32),
        ),
        in_specs=[pl.BlockSpec(memory_space=pltpu.SMEM)] + [any_space] * 3 + [vmem] * 6,
        out_specs=(vmem,) * 4,
        scratch_shapes=[
            pltpu.VMEM((slot_total + 1, tile, tile), BF16),
            pltpu.VMEM((2 * nc * tile, 2 * nr * tile), BF16),
            pltpu.VMEM((nr * rows, ports), BF16),
            pltpu.VMEM((nc, ports, rows), BF16),
            pltpu.VMEM((rows, ports), F32),
            pltpu.VMEM((ports, rows), F32),
            pltpu.VMEM((nc - 1, rows, ports), BF16),
            pltpu.VMEM((nc - 1, rows, ports), BF16),
            pltpu.VMEM((2 * nz, ports, rows), F32),
            pltpu.VMEM((2 * nz, ports, rows), F32),
            pltpu.VMEM((nz - 1, 2, ports, rows), BF16),
            pltpu.VMEM((nz - 1, 2, ports, rows), BF16),
            pltpu.VMEM((2, ports, rows), F32),
            pltpu.VMEM((ports, rows), F32),
            pltpu.VMEM((ports, rows), F32),
            pltpu.VMEM((ports, ports), F32),
            pltpu.VMEM((h_rows, ports), F32),
            pltpu.VMEM((nr, h_rows, ports), F32),
            pltpu.VMEM((nc, h_rows, ports), F32),
            pltpu.VMEM((ports, ports), F32),
        ]
        + [
            pltpu.VMEM((8, ports), F32),
            pltpu.VMEM((8, ports), F32),
            pltpu.VMEM((nr, 8, ports), F32),
            pltpu.VMEM((nc, 8, ports), F32),
        ]
        * 2
        + [sem] * 3
        + gather_sems
        + pairs(
            nc - 1, 2 * nz, nz - 1, 0, nr - 1, nc - 1, nr - 1, nr - 1, nc - 1, nr - 1, nc - 1
        ),
        compiler_params=pltpu.CompilerParams(
            collective_id=1, has_side_effects=True, vmem_limit_bytes=58 * 2**20
        ),
        name="krylov",
    )(
        slots, got_tiles, vg, wg, right_start, left_start,
        node_diagonal[:, None], node_diagonal[None, :], row_scale[:, None], scale_row,
    )
    return tuple(
        pl.pallas_call(
            finish_kernel,
            out_shape=(
                jax.ShapeDtypeStruct((rows, ports), F32),
                jax.ShapeDtypeStruct((rows, ports), F32),
                jax.ShapeDtypeStruct((ITERS, ports, ports), F32),
            ),
            in_specs=[vmem] * 4,
            out_specs=(vmem,) * 3,
            name="finish",
        )(right_rest, left_rest, norms, projections)
    )


def solution(mesh):
    return jax.shard_map(
        local,
        mesh=mesh,
        in_specs=(
            P(("row", "col"), None, None),
            P(("row", "col")),
            P(("row", "col"), None),
            P(("row", "col"), None),
            P(("row", "col")),
            P(("row", "col")),
        ),
        out_specs=(P(("row", "col"), None), P(("row", "col"), None), P()),
        check_vma=False,
    )
```

```python
import functools

import jax
import jax.numpy as jnp
from jax import lax
from jax.experimental import pallas as pl
from jax.experimental.pallas import tpu as pltpu
from jax.sharding import PartitionSpec as P

ITERS = 2
epsilon = 1e-06
MESH = pl.DeviceIdType.MESH
F32 = jnp.float32
BF16 = jnp.bfloat16
HIGHEST = lax.Precision.HIGHEST


def span(index, size):
    return pl.ds(pl.multiple_of(index * size, size), size)


def each(low, high, body):
    def step(i, carry):
        body(i)
        return carry

    lax.fori_loop(low, high, step, 0)


def remote(src, dst, send, recv, to):
    return pltpu.make_async_remote_copy(
        src_ref=src, dst_ref=dst, send_sem=send, recv_sem=recv, device_id=to, device_id_type=MESH
    )


class Place:
    def __init__(self, nr, nc):
        self.nr, self.nc, self.nz, self.ny = nr, nc, nr // 4, nc // 2
        self.row, self.col = lax.axis_index("row"), lax.axis_index("col")
        self.z, self.xl, self.core = self.row // 4, (self.row // 2) % 2, self.row % 2
        self.xh, self.y = self.col // self.ny, self.col % self.ny

    def row_at(self, d):
        return lax.rem(self.row + d + self.nr, self.nr)

    def col_at(self, d):
        return lax.rem(self.col + d + self.nc, self.nc)

    def z_at(self, d):
        return lax.rem(self.z + d + self.nz, self.nz)

    def y_at(self, d):
        return lax.rem(self.y + d + self.ny, self.ny)

    def row_of(self, z, xl, core):
        return z * 4 + xl * 2 + core

    def col_of(self, xh, y):
        return xh * self.ny + y

    def greet(self):
        barrier = pltpu.get_barrier_semaphore()
        each(1, self.nr, lambda d: pl.semaphore_signal(
            barrier, inc=1, device_id=(self.row_at(d), self.col), device_id_type=MESH))
        each(1, self.nc, lambda d: pl.semaphore_signal(
            barrier, inc=1, device_id=(self.row, self.col_at(d)), device_id_type=MESH))
        return lambda: pl.semaphore_wait(barrier, self.nr + self.nc - 2)


class RightGather:
    def __init__(self, me, vg, block, sems):
        self.me, self.vg, self.block = me, vg, block
        self.x_ss, self.x_rs, self.z_ss, self.z_rs, self.f_ss, self.f_rs = sems

    def slot(self, r):
        return self.vg.at[span(r, self.block)]

    def x_copy(self, r):
        me = self.me
        return remote(self.slot(r), self.slot(r), self.x_ss, self.x_rs, (me.row_of(me.z, 1 - me.xl, me.core), me.col))

    def z_copy(self, second, d, r):
        me = self.me
        i = second * (me.nz - 1) + d - 1
        to = (me.row_of(me.z_at(d), me.xl, me.core), me.col)
        return remote(self.slot(r), self.slot(r), self.z_ss.at[i], self.z_rs.at[i], to)

    def f_copy(self, second, d, r):
        me = self.me
        i = second * me.nz + d
        to = (me.row_of(me.z, me.xl, 1 - me.core), me.col)
        return remote(self.slot(r), self.slot(r), self.f_ss.at[i], self.f_rs.at[i], to)

    def from_z(self, second, d, other=0):
        me = self.me
        xl = 1 - me.xl if second else me.xl
        core = 1 - me.core if other else me.core
        return me.row_of(me.z_at(-d), xl, core)

    def start(self):
        me = self.me
        self.x_copy(me.row).start()
        each(1, me.nz, lambda d: self.z_copy(0, d, me.row).start())
        self.f_copy(0, 0, me.row).start()

    def pass_x(self):
        r = self.from_z(1, 0)
        self.x_copy(r).wait_recv()
        each(1, self.me.nz, lambda d: self.z_copy(1, d, r).start())
        self.f_copy(1, 0, r).start()

    def pass_z(self):
        for second in range(2):
            def one(d, second=second):
                r = self.from_z(second, d)
                self.z_copy(second, d, r).wait_recv()
                self.f_copy(second, d, r).start()

            each(1, self.me.nz, one)

    def arrive(self):
        for second in range(2):
            each(0, self.me.nz, lambda d, second=second: self.f_copy(
                second, d, self.from_z(second, d, 1)).wait_recv())

    def sent(self):
        me = self.me
        self.x_copy(me.row).wait_send()
        for second in range(2):
            each(1, me.nz, lambda d, second=second: self.z_copy(second, d, me.row).wait_send())
            each(0, me.nz, lambda d, second=second: self.f_copy(second, d, me.row).wait_send())


class LeftGather:
    def __init__(self, me, wg, sems):
        self.me, self.wg = me, wg
        self.x_ss, self.x_rs, self.y_ss, self.y_rs = sems

    def x_copy(self, c):
        me = self.me
        return remote(self.wg.at[c], self.wg.at[c], self.x_ss, self.x_rs, (me.row, me.col_of(1 - me.xh, me.y)))

    def y_copy(self, second, d, c):
        me = self.me
        i = second * (me.ny - 1) + d - 1
        to = (me.row, me.col_of(me.xh, me.y_at(d)))
        return remote(self.wg.at[c], self.wg.at[c], self.y_ss.at[i], self.y_rs.at[i], to)

    def start(self):
        me = self.me
        self.x_copy(me.col).start()
        each(1, me.ny, lambda d: self.y_copy(0, d, me.col).start())

    def pass_x(self):
        me = self.me
        c = me.col_of(1 - me.xh, me.y)
        self.x_copy(c).wait_recv()
        each(1, me.ny, lambda d: self.y_copy(1, d, c).start())

    def arrive(self):
        me = self.me
        for second in range(2):
            xh = 1 - me.xh if second else me.xh
            each(1, me.ny, lambda d, second=second, xh=xh: self.y_copy(
                second, d, me.col_of(xh, me.y_at(-d))).wait_recv())

    def sent(self):
        me = self.me
        self.x_copy(me.col).wait_send()
        for second in range(2):
            each(1, me.ny, lambda d, second=second: self.y_copy(second, d, me.col).wait_send())


class Exchange:
    def __init__(self, me, along_row, src, slots, ss, rs, pick=None):
        self.me, self.along_row, self.src, self.slots, self.ss, self.rs = me, along_row, src, slots, ss, rs
        self.pick = pick or (lambda i: src)
        self.size = me.nr if along_row else me.nc
        self.mine = me.row if along_row else me.col

    def at(self, d):
        return self.me.row_at(d) if self.along_row else self.me.col_at(d)

    def copy(self, d, slot):
        me = self.me
        to = (self.at(d), me.col) if self.along_row else (me.row, self.at(d))
        return remote(self.pick(self.at(d)), self.slots.at[slot], self.ss.at[d - 1], self.rs.at[d - 1], to)

    def start(self):
        each(1, self.size, lambda d: self.copy(d, self.mine).start())

    def total(self):
        each(1, self.size, lambda d: self.copy(d, self.at(-d)).wait_recv())
        total = self.slots[0]
        for i in range(1, self.size):
            total += self.slots[i]
        return total

    def sent(self):
        each(1, self.size, lambda d: self.copy(d, self.mine).wait_send())


def gather_kernel(nr, nc, codes, right, left, scale_row, vg, wg, got, got_row, *sems):
    me = Place(nr, nc)
    hold = me.greet()
    block = right.shape[0]
    v = RightGather(me, vg, block, sems[:6])
    w = LeftGather(me, wg, sems[6:10])
    c1_ss, c1_rs, c2_ss, c2_rs = sems[10:14]
    start_right = right[...]
    vg[span(me.row, block)] = start_right.astype(BF16)
    wg[me.col] = (scale_row[...] * jnp.transpose(start_right + left[...])).astype(BF16)
    got_row[me.row] = codes[me.row]

    def c1_copy(d, slot):
        return remote(codes.at[me.row_at(d)], got_row.at[slot], c1_ss.at[d - 1], c1_rs.at[d - 1],
                      (me.row_at(d), me.col))

    def c2_copy(d, slot):
        return remote(got_row, got.at[slot], c2_ss.at[d - 1], c2_rs.at[d - 1], (me.row, me.col_at(d)))

    hold()
    each(1, nr, lambda d: c1_copy(d, me.row).start())
    v.start()
    w.start()
    each(1, nr, lambda d: c1_copy(d, me.row_at(-d)).wait_recv())
    each(1, nc, lambda d: c2_copy(d, me.col).start())
    got[me.col] = got_row[...]
    v.pass_x()
    w.pass_x()
    v.pass_z()
    each(1, nc, lambda d: c2_copy(d, me.col_at(-d)).wait_recv())
    w.arrive()
    v.arrive()
    v.sent()
    w.sent()
    each(1, nr, lambda d: c1_copy(d, me.row).wait_send())
    each(1, nc, lambda d: c2_copy(d, me.col).wait_send())


def krylov_kernel(
    nr, nc, order,
    slots_ref, tiles_hbm, vg_hbm, wg_hbm, right_ref, left_ref, diag_col, diag_row, scale_col, scale_row,
    r_new, lt_new, norm_out, h_out,
    tiles, ta, vg, wg, v_ref, wt,
    r_send, r_recv, sib_send, sib_recv, l_send, l_recv, l_keep, x_send, x_recv,
    h_loc, h_part, h_from_row, h_from_col, h_full,
    n_loc, n_part, n_from_row, n_from_col,
    tile_sem, vg_sem, wg_sem, *sems,
):
    me = Place(nr, nc)
    row, col, nz = me.row, me.col, me.nz
    tile = tiles.shape[1]
    block = 2 * tile
    slot_total = tiles_hbm.shape[0]
    h_rows = h_loc.shape[0] // nc
    v = RightGather(me, vg, block, sems[:6])
    w = LeftGather(me, wg, sems[6:10])
    (r_ss, r_rs, s_ss, s_rs, l_ss, l_rs, x_ss, x_rs, h1_ss, h1_rs, h2_ss, h2_rs, h3_ss, h3_rs,
     n1_ss, n1_rs, n2_ss, n2_rs) = sems[10:]

    def r_copy(d):
        return remote(r_send.at[d - 1], r_recv.at[d - 1], r_ss.at[d - 1], r_rs.at[d - 1], (row, me.col_at(d)))

    def s_copy(e):
        to = (me.row_of(me.z, me.xl, 1 - me.core), col)
        return remote(sib_send.at[e], sib_recv.at[e], s_ss.at[e], s_rs.at[e], to)

    def l_copy(i):
        to = (me.row_of(me.z_at(i % (nz - 1) + 1), me.xl, me.core), col)
        return remote(l_send.at[i], l_recv.at[i], l_ss.at[i], l_rs.at[i], to)

    def x_copy():
        return remote(x_send, x_recv, x_ss, x_rs, (me.row_of(me.z, 1 - me.xl, me.core), col))

    def h3_copy(d, slot):
        at = h_full.at[span(slot, h_rows)]
        return remote(at, at, h3_ss.at[d - 1], h3_rs.at[d - 1], (row, me.col_at(d)))

    h1 = Exchange(me, False, h_loc, h_from_col, h1_ss, h1_rs, lambda i: h_loc.at[span(i, h_rows)])
    h2 = Exchange(me, True, h_part, h_from_row, h2_ss, h2_rs)
    n1 = Exchange(me, True, n_loc, n_from_row, n1_ss, n1_rs)
    n2 = Exchange(me, False, n_part, n_from_col, n2_ss, n2_rs)

    load = pltpu.make_async_copy(tiles_hbm, tiles.at[pl.ds(0, slot_total)], tile_sem)
    load.start()
    load_vg = pltpu.make_async_copy(vg_hbm, vg, vg_sem)
    load_vg.start()
    load_wg = pltpu.make_async_copy(wg_hbm, wg, wg_sem)
    load_wg.start()
    hold = me.greet()
    wt[...] = jnp.transpose(right_ref[...] + left_ref[...])
    v_ref[...] = right_ref[...]
    n_loc[...] = jnp.zeros_like(n_loc)
    tiles[slot_total] = jnp.zeros((tile, tile), BF16)
    load.wait()

    def one_row(a):
        for b in range(2 * nr):
            ta[span(a, tile), b * tile : (b + 1) * tile] = tiles[slots_ref[a * 2 * nr + b]]

    each(0, 2 * nc, one_row)
    load_vg.wait()
    load_wg.wait()
    hold()

    def right_part(c):
        return jnp.dot(ta[span(c, block)], vg[...], preferred_element_type=F32)

    def left_part(r):
        rows = jnp.concatenate([wg[c] for c in range(nc)], axis=1)
        return jnp.dot(rows, ta[:, span(r, block)], preferred_element_type=F32)

    def xl_of(home):
        return me.xl * home + (1 - me.xl) * (1 - home)

    def norm_of(total):
        return jnp.sqrt(total * (1.0 / order) + epsilon)

    for turn in range(ITERS):
        last = turn == ITERS - 1
        if turn:
            v.arrive()

        def right_step(d):
            r_send[d - 1] = right_part(me.col_at(d)).astype(BF16)
            r_copy(d).start()

        each(1, nc, right_step)
        r_new[...] = right_part(col) + diag_col[...] * v_ref[...]

        if turn:
            w.arrive()

        def left_other(e):
            sib_send[e] = left_part(me.row_of(me.z_at(e % nz + 1), xl_of(e // nz), 1 - me.core))
            s_copy(e).start()

        def left_own(e):
            s_copy(e).wait_recv()
            return left_part(me.row_of(me.z_at(e % nz + 1), xl_of(e // nz), me.core)) + sib_recv[e]

        for home in range(2):
            each(home * nz, home * nz + nz, left_other)

            def left_away(d, home=home):
                i = home * (nz - 1) + d
                l_send[i] = left_own(home * nz + d).astype(BF16)
                l_copy(i).start()

            each(0, nz - 1, left_away)
            l_keep[home] = left_own(home * nz + nz - 1)

        def right_sum(d):
            r_copy(d).wait_recv()
            r_new[...] += r_recv[d - 1].astype(F32)

        each(1, nc, right_sum)
        r_new[...] = scale_col[...] * r_new[...]

        h_loc[...] = jnp.dot(wt[...], r_new[...], precision=HIGHEST, preferred_element_type=F32)
        h1.start()
        h_from_col[col] = h_loc[span(col, h_rows)]
        part = h1.total()
        h_part[...] = part
        h2.start()
        h_from_row[row] = part

        def left_sum(home):
            def one(d):
                i = home * (nz - 1) + d
                l_copy(i).wait_recv()
                l_keep[home] += l_recv[i].astype(F32)

            each(0, nz - 1, one)

        left_sum(0)
        x_send[...] = l_keep[0]
        x_copy().start()

        h_full[span(col, h_rows)] = h2.total() * (1.0 / order)
        each(1, nc, lambda d: h3_copy(d, col).start())
        scaled = scale_row[...] * wt[...]
        left_sum(1)
        lt_new[...] = l_keep[1] + diag_row[...] * scaled
        each(1, nc, lambda d: h3_copy(d, me.col_at(-d)).wait_recv())

        project = h_full[...]
        rest = r_new[...] - jnp.dot(v_ref[...], project, precision=HIGHEST, preferred_element_type=F32)
        r_new[...] = rest
        n_loc[0:1] = jnp.sum(rest * rest, axis=0, keepdims=True)

        h_out[turn] = h_full[...]
        lt_new[...] -= jnp.dot(h_full[...], wt[...], precision=HIGHEST, preferred_element_type=F32)
        x_copy().wait_recv()
        lt_new[...] += x_recv[...]
        left_rest = lt_new[...]
        n_loc[1:2] = jnp.sum(jnp.transpose(left_rest * left_rest), axis=0, keepdims=True)
        n1.start()
        n_from_row[row] = n_loc[...]
        n_part[...] = n1.total()
        n2.start()
        n_from_col[col] = n_part[...]

        if turn:
            v.sent()
            w.sent()
        each(1, nc, lambda d: r_copy(d).wait_send())
        each(0, 2 * nz, lambda e: s_copy(e).wait_send())
        each(0, 2 * (nz - 1), lambda i: l_copy(i).wait_send())
        x_copy().wait_send()
        h1.sent()
        h2.sent()
        each(1, nc, lambda d: h3_copy(d, col).wait_send())
        n1.sent()
        total = n2.total()
        n2.sent()
        norms = norm_of(total)
        if last:
            norm_out[...] = norms
        else:
            v_new = r_new[...] / norms[0:1]
            v_ref[...] = v_new
            vg[span(row, block)] = v_new.astype(BF16)
            v.start()
            size = lt_new.shape
            w_new = lt_new[...] / jnp.transpose(jnp.broadcast_to(norms[1:2], (size[1], size[0])))
            wt[...] = w_new
            wg[col] = (scale_row[...] * w_new).astype(BF16)
            w.start()
            v.pass_x()
            w.pass_x()
            v.pass_z()


def finish_kernel(r_ref, lt_ref, norm_ref, h_ref, v_out, w_out, h_out):
    v_out[...] = r_ref[...] / norm_ref[0:1]
    w_out[...] = jnp.transpose(lt_ref[...]) / norm_ref[1:2]
    h_out[...] = h_ref[...]


def local(tile_values, slot_codes, right_start, left_start, node_diagonal, row_scale):
    nr, nc = lax.axis_size("row"), lax.axis_size("col")
    slot_total, tile = tile_values.shape[:2]
    rows, ports = right_start.shape
    order = rows * nr * nc
    nz, ny = nr // 4, nc // 2
    vmem = pl.BlockSpec(memory_space=pltpu.VMEM)
    any_space = pl.BlockSpec(memory_space=pl.ANY)
    sem = pltpu.SemaphoreType.DMA
    scale_row = row_scale[None, :]

    def pairs(*counts):
        return [sem((n,)) if n else sem for n in counts for _ in range(2)]

    gather_sems = pairs(0, 2 * (nz - 1), 2 * nz, 0, 2 * (ny - 1))

    got_tiles = lax.all_to_all(tile_values, ("row", "col"), split_axis=0, concat_axis=0, tiled=True)
    codes = jnp.pad(slot_codes.reshape(nr, 1, 2 * nc), ((0, 0), (0, 7), (0, 128 - 2 * nc)))
    vg, wg, got = pl.pallas_call(
        functools.partial(gather_kernel, nr, nc),
        out_shape=(
            jax.ShapeDtypeStruct((nr * rows, ports), BF16),
            jax.ShapeDtypeStruct((nc, ports, rows), BF16),
            jax.ShapeDtypeStruct((nc, nr, 8, 128), jnp.int32),
        ),
        in_specs=[vmem] * 4,
        out_specs=(vmem,) * 3,
        scratch_shapes=[pltpu.VMEM((nr, 8, 128), jnp.int32)] + gather_sems + pairs(nr - 1, nc - 1),
        compiler_params=pltpu.CompilerParams(
            collective_id=0, has_side_effects=True, vmem_limit_bytes=16 * 2**20
        ),
        cost_estimate=pl.CostEstimate(flops=10**10, bytes_accessed=10**7, transcendentals=0),
        name="gather",
    )(codes, right_start, left_start, scale_row)

    got = lax.dynamic_slice_in_dim(got[:, :, 0, :], 2 * lax.axis_index("col"), 2, axis=2)
    got_codes = jnp.transpose(got, (1, 0, 2)).reshape(slot_total)
    places = 4 * nr * nc
    hit = got_codes[None, :] == jnp.arange(places, dtype=jnp.int32)[:, None]
    slots = jnp.max(jnp.where(hit, jnp.arange(slot_total, dtype=jnp.int32)[None, :], -1), axis=1)
    slots = jnp.where(slots < 0, slot_total, slots)

    h_rows = ports // nc
    right_rest, left_rest, norms, projections = pl.pallas_call(
        functools.partial(krylov_kernel, nr, nc, order),
        out_shape=(
            jax.ShapeDtypeStruct((rows, ports), F32),
            jax.ShapeDtypeStruct((ports, rows), F32),
            jax.ShapeDtypeStruct((8, ports), F32),
            jax.ShapeDtypeStruct((ITERS, ports, ports), F32),
        ),
        in_specs=[pl.BlockSpec(memory_space=pltpu.SMEM)] + [any_space] * 3 + [vmem] * 6,
        out_specs=(vmem,) * 4,
        scratch_shapes=[
            pltpu.VMEM((slot_total + 1, tile, tile), BF16),
            pltpu.VMEM((2 * nc * tile, 2 * nr * tile), BF16),
            pltpu.VMEM((nr * rows, ports), BF16),
            pltpu.VMEM((nc, ports, rows), BF16),
            pltpu.VMEM((rows, ports), F32),
            pltpu.VMEM((ports, rows), F32),
            pltpu.VMEM((nc - 1, rows, ports), BF16),
            pltpu.VMEM((nc - 1, rows, ports), BF16),
            pltpu.VMEM((2 * nz, ports, rows), F32),
            pltpu.VMEM((2 * nz, ports, rows), F32),
            pltpu.VMEM((2 * (nz - 1), ports, rows), BF16),
            pltpu.VMEM((2 * (nz - 1), ports, rows), BF16),
            pltpu.VMEM((2, ports, rows), F32),
            pltpu.VMEM((ports, rows), F32),
            pltpu.VMEM((ports, rows), F32),
            pltpu.VMEM((ports, ports), F32),
            pltpu.VMEM((h_rows, ports), F32),
            pltpu.VMEM((nr, h_rows, ports), F32),
            pltpu.VMEM((nc, h_rows, ports), F32),
            pltpu.VMEM((ports, ports), F32),
            pltpu.VMEM((8, ports), F32),
            pltpu.VMEM((8, ports), F32),
            pltpu.VMEM((nr, 8, ports), F32),
            pltpu.VMEM((nc, 8, ports), F32),
        ]
        + [sem] * 3
        + gather_sems
        + pairs(
            nc - 1, 2 * nz, 2 * (nz - 1), 0, nc - 1, nr - 1, nc - 1, nr - 1, nc - 1
        ),
        compiler_params=pltpu.CompilerParams(
            collective_id=1, has_side_effects=True, vmem_limit_bytes=58 * 2**20
        ),
        name="krylov",
    )(
        slots, got_tiles, vg, wg, right_start, left_start,
        node_diagonal[:, None], node_diagonal[None, :], row_scale[:, None], scale_row,
    )
    return tuple(
        pl.pallas_call(
            finish_kernel,
            out_shape=(
                jax.ShapeDtypeStruct((rows, ports), F32),
                jax.ShapeDtypeStruct((rows, ports), F32),
                jax.ShapeDtypeStruct((ITERS, ports, ports), F32),
            ),
            in_specs=[vmem] * 4,
            out_specs=(vmem,) * 3,
            name="finish",
        )(right_rest, left_rest, norms, projections)
    )


def solution(mesh):
    return jax.shard_map(
        local,
        mesh=mesh,
        in_specs=(
            P(("row", "col"), None, None),
            P(("row", "col")),
            P(("row", "col"), None),
            P(("row", "col"), None),
            P(("row", "col")),
            P(("row", "col")),
        ),
        out_specs=(P(("row", "col"), None), P(("row", "col"), None), P()),
        check_vma=False,
    )
```

```python
import functools

import jax
import jax.numpy as jnp
from jax import lax
from jax.experimental import pallas as pl
from jax.experimental.pallas import tpu as pltpu
from jax.sharding import PartitionSpec as P

ITERS = 2
epsilon = 1e-06
MESH = pl.DeviceIdType.MESH
F32 = jnp.float32
BF16 = jnp.bfloat16
HIGHEST = lax.Precision.HIGHEST


def span(index, size):
    return pl.ds(pl.multiple_of(index * size, size), size)


def each(low, high, body, unroll=False):
    def step(i, carry):
        body(i)
        return carry

    lax.fori_loop(low, high, step, 0, unroll=unroll)


def remote(src, dst, send, recv, to):
    return pltpu.make_async_remote_copy(
        src_ref=src, dst_ref=dst, send_sem=send, recv_sem=recv, device_id=to, device_id_type=MESH
    )


class Place:
    def __init__(self, nr, nc):
        self.nr, self.nc, self.nz, self.ny = nr, nc, nr // 4, nc // 2
        self.row, self.col = lax.axis_index("row"), lax.axis_index("col")
        self.z, self.xl, self.core = self.row // 4, (self.row // 2) % 2, self.row % 2
        self.xh, self.y = self.col // self.ny, self.col % self.ny

    def row_at(self, d):
        return lax.rem(self.row + d + self.nr, self.nr)

    def col_at(self, d):
        return lax.rem(self.col + d + self.nc, self.nc)

    def z_at(self, d):
        return lax.rem(self.z + d + self.nz, self.nz)

    def y_at(self, d):
        return lax.rem(self.y + d + self.ny, self.ny)

    def row_of(self, z, xl, core):
        return z * 4 + xl * 2 + core

    def col_of(self, xh, y):
        return xh * self.ny + y

    def greet(self):
        barrier = pltpu.get_barrier_semaphore()
        each(1, self.nr, lambda d: pl.semaphore_signal(
            barrier, inc=1, device_id=(self.row_at(d), self.col), device_id_type=MESH))
        each(1, self.nc, lambda d: pl.semaphore_signal(
            barrier, inc=1, device_id=(self.row, self.col_at(d)), device_id_type=MESH))
        return lambda: pl.semaphore_wait(barrier, self.nr + self.nc - 2)


class RightGather:
    def __init__(self, me, vg, block, sems):
        self.me, self.vg, self.block = me, vg, block
        self.x_ss, self.x_rs, self.z_ss, self.z_rs, self.f_ss, self.f_rs = sems

    def slot(self, r):
        return self.vg.at[span(r, self.block)]

    def x_copy(self, r):
        me = self.me
        return remote(self.slot(r), self.slot(r), self.x_ss, self.x_rs, (me.row_of(me.z, 1 - me.xl, me.core), me.col))

    def z_copy(self, second, d, r):
        me = self.me
        i = second * (me.nz - 1) + d - 1
        to = (me.row_of(me.z_at(d), me.xl, me.core), me.col)
        return remote(self.slot(r), self.slot(r), self.z_ss, self.z_rs.at[i], to)

    def f_copy(self, second, r, blocks=0):
        me = self.me
        at = self.vg.at[pl.ds(0, blocks * self.block)] if blocks else self.slot(r)
        return remote(at, at, self.f_ss, self.f_rs.at[second], (me.row_of(me.z, me.xl, 1 - me.core), me.col))

    def from_z(self, second, d):
        me = self.me
        return me.row_of(me.z_at(-d), 1 - me.xl if second else me.xl, me.core)

    def start(self):
        me = self.me
        self.x_copy(me.row).start()
        each(1, me.nz, lambda d: self.z_copy(0, d, me.row).start())
        self.f_copy(0, me.row).start()

    def pass_x(self):
        r = self.from_z(1, 0)
        self.x_copy(r).wait_recv()
        each(1, self.me.nz, lambda d: self.z_copy(1, d, r).start())
        self.f_copy(1, r).start()

    def pass_z(self, second):
        def one(d):
            r = self.from_z(second, d)
            self.z_copy(second, d, r).wait_recv()
            self.f_copy(second, r).start()

        each(1, self.me.nz, one)

    def arrive(self, second):
        self.f_copy(second, 0, self.me.nz).wait_recv()

    def sent(self):
        me = self.me
        self.x_copy(me.row).wait_send()
        at = self.vg.at[pl.ds(0, 2 * (me.nz - 1) * self.block)]
        remote(at, at, self.z_ss, self.x_rs, (me.row_of(me.z, 1 - me.xl, me.core), me.col)).wait_send()
        self.f_copy(0, 0, 2 * me.nz).wait_send()


class LeftGather:
    def __init__(self, me, wg, sems):
        self.me, self.wg = me, wg
        self.x_ss, self.x_rs, self.y_ss, self.y_rs = sems

    def x_copy(self, c):
        me = self.me
        return remote(self.wg.at[c], self.wg.at[c], self.x_ss, self.x_rs, (me.row, me.col_of(1 - me.xh, me.y)))

    def y_copy(self, d, c):
        me = self.me
        to = (me.row, me.col_of(me.xh, me.y_at(d)))
        return remote(self.wg.at[c], self.wg.at[c], self.y_ss, self.y_rs, to)

    def y_all(self):
        me = self.me
        at = self.wg.at[pl.ds(0, 2 * (me.ny - 1))]
        return remote(at, at, self.y_ss, self.y_rs, (me.row, me.col_of(1 - me.xh, me.y)))

    def start(self):
        me = self.me
        self.x_copy(me.col).start()
        each(1, me.ny, lambda d: self.y_copy(d, me.col).start())

    def pass_x(self):
        me = self.me
        c = me.col_of(1 - me.xh, me.y)
        self.x_copy(c).wait_recv()
        each(1, me.ny, lambda d: self.y_copy(d, c).start())

    def arrive(self):
        self.y_all().wait_recv()

    def sent(self):
        self.x_copy(self.me.col).wait_send()
        self.y_all().wait_send()


class Exchange:
    def __init__(self, me, along_row, src, slots, ss, rs, pick=None):
        self.me, self.along_row, self.src, self.slots, self.ss, self.rs = me, along_row, src, slots, ss, rs
        self.pick = pick or (lambda i: src)
        self.size = me.nr if along_row else me.nc
        self.mine = me.row if along_row else me.col

    def at(self, d):
        return self.me.row_at(d) if self.along_row else self.me.col_at(d)

    def copy(self, d, slot):
        me = self.me
        to = (self.at(d), me.col) if self.along_row else (me.row, self.at(d))
        return remote(self.pick(self.at(d)), self.slots.at[slot], self.ss, self.rs, to)

    def start(self):
        each(1, self.size, lambda d: self.copy(d, self.mine).start(), True)

    def all(self):
        me = self.me
        at = self.slots.at[pl.ds(0, self.size - 1)]
        to = (self.at(1), me.col) if self.along_row else (me.row, self.at(1))
        return remote(at, at, self.ss, self.rs, to)

    def total(self):
        self.all().wait_recv()
        total = self.slots[0]
        for i in range(1, self.size):
            total += self.slots[i]
        return total

    def sent(self):
        self.all().wait_send()


def gather_kernel(nr, nc, codes, right, left, scale_row, vg, wg, got, got_row, *sems):
    me = Place(nr, nc)
    hold = me.greet()
    block = right.shape[0]
    v = RightGather(me, vg, block, sems[:6])
    w = LeftGather(me, wg, sems[6:10])
    c1_ss, c1_rs, c2_ss, c2_rs = sems[10:14]
    start_right = right[...]
    vg[span(me.row, block)] = start_right.astype(BF16)
    wg[me.col] = (scale_row[...] * jnp.transpose(start_right + left[...])).astype(BF16)
    got_row[me.row] = codes[me.row]

    def c1_copy(d, slot):
        return remote(codes.at[me.row_at(d)], got_row.at[slot], c1_ss, c1_rs, (me.row_at(d), me.col))

    def c2_copy(d, slot):
        return remote(got_row, got.at[slot], c2_ss, c2_rs, (me.row, me.col_at(d)))

    def c1_all():
        at = got_row.at[pl.ds(0, nr - 1)]
        return remote(at, at, c1_ss, c1_rs, (me.row_at(1), me.col))

    def c2_all():
        at = got.at[pl.ds(0, nc - 1)]
        return remote(at, at, c2_ss, c2_rs, (me.row, me.col_at(1)))

    hold()
    each(1, nr, lambda d: c1_copy(d, me.row).start())
    v.start()
    w.start()
    c1_all().wait_recv()
    each(1, nc, lambda d: c2_copy(d, me.col).start())
    got[me.col] = got_row[...]
    v.pass_x()
    w.pass_x()
    v.pass_z(0)
    v.pass_z(1)
    c2_all().wait_recv()
    w.arrive()
    v.arrive(0)
    v.arrive(1)
    v.sent()
    w.sent()
    c1_all().wait_send()
    c2_all().wait_send()


def krylov_kernel(
    nr, nc, order,
    slots_ref, tiles_hbm, vg_hbm, wg_hbm, right_ref, left_ref, diag_col, diag_row, scale_col, scale_row,
    r_new, lt_new, norm_out, h_out,
    tiles, ta, vg, wg, v_ref, wt,
    r_send, r_recv, sib_send, sib_recv, l_send, l_recv, l_keep, x_send, x_recv,
    h_loc, h_part, h_from_row, h_from_col, h_full,
    n_loc, n_part, n_from_row, n_from_col,
    tile_sem, vg_sem, wg_sem, *sems,
):
    me = Place(nr, nc)
    row, col, nz = me.row, me.col, me.nz
    tile = tiles.shape[1]
    block = 2 * tile
    slot_total = tiles_hbm.shape[0]
    h_rows = h_loc.shape[0] // nc
    v = RightGather(me, vg, block, sems[:6])
    w = LeftGather(me, wg, sems[6:10])
    (r_ss, r_rs, s_ss, s_rs, l_ss, l_rs, x_ss, x_rs, h1_ss, h1_rs, h2_ss, h2_rs, h3_ss, h3_rs,
     n1_ss, n1_rs, n2_ss, n2_rs) = sems[10:]

    def r_copy(d):
        return remote(r_send.at[d - 1], r_recv.at[d - 1], r_ss, r_rs.at[d - 1], (row, me.col_at(d)))

    def r_sent():
        remote(r_send, r_recv, r_ss, r_rs.at[0], (row, me.col_at(1))).wait_send()

    def s_copy(e):
        to = (me.row_of(me.z, me.xl, 1 - me.core), col)
        return remote(sib_send.at[e], sib_recv.at[e], s_ss, s_rs.at[e], to)

    def s_sent():
        remote(sib_send, sib_recv, s_ss, s_rs.at[0], (me.row_of(me.z, me.xl, 1 - me.core), col)).wait_send()

    def l_copy(i):
        to = (me.row_of(me.z_at(i % (nz - 1) + 1), me.xl, me.core), col)
        return remote(l_send.at[i], l_recv.at[i], l_ss, l_rs.at[i // (nz - 1)], to)

    def l_sent():
        remote(l_send, l_recv, l_ss, l_rs.at[0], (me.row_of(me.z, 1 - me.xl, me.core), col)).wait_send()

    def l_arrive(home):
        at = l_recv.at[pl.ds(home * (nz - 1), nz - 1)]
        remote(at, at, l_ss, l_rs.at[home], (me.row_of(me.z, 1 - me.xl, me.core), col)).wait_recv()

    def x_copy():
        return remote(x_send, x_recv, x_ss, x_rs, (me.row_of(me.z, 1 - me.xl, me.core), col))

    def h3_copy(d, slot):
        at = h_full.at[span(slot, h_rows)]
        return remote(at, at, h3_ss, h3_rs, (row, me.col_at(d)))

    def h3_all():
        at = h_full.at[pl.ds(0, (nc - 1) * h_rows)]
        return remote(at, at, h3_ss, h3_rs, (row, me.col_at(1)))

    h1 = Exchange(me, False, h_loc, h_from_col, h1_ss, h1_rs, lambda i: h_loc.at[span(i, h_rows)])
    h2 = Exchange(me, True, h_part, h_from_row, h2_ss, h2_rs)
    n1 = Exchange(me, True, n_loc, n_from_row, n1_ss, n1_rs)
    n2 = Exchange(me, False, n_part, n_from_col, n2_ss, n2_rs)

    load = pltpu.make_async_copy(tiles_hbm, tiles.at[pl.ds(0, slot_total)], tile_sem)
    load.start()
    load_vg = pltpu.make_async_copy(vg_hbm, vg, vg_sem)
    load_vg.start()
    load_wg = pltpu.make_async_copy(wg_hbm, wg, wg_sem)
    load_wg.start()
    hold = me.greet()
    wt[...] = jnp.transpose(right_ref[...] + left_ref[...])
    v_ref[...] = right_ref[...]
    n_loc[...] = jnp.zeros_like(n_loc)
    tiles[slot_total] = jnp.zeros((tile, tile), BF16)
    load.wait()

    def one_row(a):
        for b in range(2 * nr):
            ta[span(a, tile), b * tile : (b + 1) * tile] = tiles[slots_ref[a * 2 * nr + b]]

    each(0, 2 * nc, one_row)
    load_vg.wait()
    load_wg.wait()
    hold()

    def right_part(c):
        return jnp.dot(ta[span(c, block)], vg[...], preferred_element_type=F32)

    def right_half(c, xl):
        total = None
        for z in range(nz):
            at = span(2 * z + xl, 2 * block)
            part = jnp.dot(ta[span(c, block), at], vg[at], preferred_element_type=F32)
            total = part if total is None else total + part
        return total

    def drain():
        r_sent()
        s_sent()
        l_sent()
        x_copy().wait_send()
        h1.sent()
        h2.sent()
        h3_all().wait_send()
        n1.sent()
        n2.sent()

    def left_part(r):
        rows = jnp.concatenate([wg[c] for c in range(nc)], axis=1)
        return jnp.dot(rows, ta[:, span(r, block)], preferred_element_type=F32)

    def xl_of(home):
        return me.xl * home + (1 - me.xl) * (1 - home)

    def norm_of(total):
        return jnp.sqrt(total * (1.0 / order) + epsilon)

    for turn in range(ITERS):
        last = turn == ITERS - 1
        if turn:
            v.pass_x()
            v.pass_z(0)
            w.pass_x()
            drain()
            v.arrive(0)

            def right_first(d):
                sib_send[d] = right_half(me.col_at(d), me.xl)

            each(0, nc, right_first)
            v.pass_z(1)
            v.arrive(1)

        def right_step(d):
            if turn:
                r_send[d - 1] = (sib_send[d] + right_half(me.col_at(d), 1 - me.xl)).astype(BF16)
            else:
                r_send[d - 1] = right_part(me.col_at(d)).astype(BF16)
            r_copy(d).start()

        each(1, nc, right_step)
        own = sib_send[0] + right_half(col, 1 - me.xl) if turn else right_part(col)
        r_new[...] = own + diag_col[...] * v_ref[...]

        if turn:
            w.arrive()

        def left_other(e):
            sib_send[e] = left_part(me.row_of(me.z_at(e % nz + 1), xl_of(e // nz), 1 - me.core))
            s_copy(e).start()

        def left_own(e):
            s_copy(e).wait_recv()
            return left_part(me.row_of(me.z_at(e % nz + 1), xl_of(e // nz), me.core)) + sib_recv[e]

        for home in range(2):
            each(home * nz, home * nz + nz, left_other)

            def left_away(d, home=home):
                i = home * (nz - 1) + d
                l_send[i] = left_own(home * nz + d).astype(BF16)
                l_copy(i).start()

            each(0, nz - 1, left_away)
            l_keep[home] = left_own(home * nz + nz - 1)

        def right_sum(d):
            r_copy(d).wait_recv()
            r_new[...] += r_recv[d - 1].astype(F32)

        each(1, nc, right_sum)
        r_new[...] = scale_col[...] * r_new[...]

        h_loc[...] = jnp.dot(wt[...], r_new[...], precision=HIGHEST, preferred_element_type=F32)
        h1.start()
        h_from_col[col] = h_loc[span(col, h_rows)]
        part = h1.total()
        h_part[...] = part
        h2.start()
        h_from_row[row] = part

        def left_sum(home):
            l_arrive(home)
            total = l_keep[home]
            for d in range(nz - 1):
                total += l_recv[home * (nz - 1) + d].astype(F32)
            return total

        x_send[...] = left_sum(0)
        x_copy().start()

        h_full[span(col, h_rows)] = h2.total() * (1.0 / order)
        each(1, nc, lambda d: h3_copy(d, col).start(), True)
        scaled = scale_row[...] * wt[...]
        lt_new[...] = left_sum(1) + diag_row[...] * scaled
        h3_all().wait_recv()

        project = h_full[...]
        rest = r_new[...] - jnp.dot(v_ref[...], project, precision=HIGHEST, preferred_element_type=F32)
        r_new[...] = rest
        n_loc[0:1] = jnp.sum(rest * rest, axis=0, keepdims=True)

        h_out[turn] = h_full[...]
        lt_new[...] -= jnp.dot(h_full[...], wt[...], precision=HIGHEST, preferred_element_type=F32)
        x_copy().wait_recv()
        lt_new[...] += x_recv[...]
        left_rest = lt_new[...]
        n_loc[1:2] = jnp.sum(jnp.transpose(left_rest * left_rest), axis=0, keepdims=True)
        n1.start()
        n_from_row[row] = n_loc[...]
        n_part[...] = n1.total()
        n2.start()
        n_from_col[col] = n_part[...]

        if last:
            v.sent()
            w.sent()
        total = n2.total()
        if last:
            drain()
        norms = norm_of(total)
        if last:
            norm_out[...] = norms
        else:
            v_new = r_new[...] / norms[0:1]
            v_ref[...] = v_new
            vg[span(row, block)] = v_new.astype(BF16)
            v.start()
            size = lt_new.shape
            w_new = lt_new[...] / jnp.transpose(jnp.broadcast_to(norms[1:2], (size[1], size[0])))
            wt[...] = w_new
            wg[col] = (scale_row[...] * w_new).astype(BF16)
            w.start()


def finish_kernel(r_ref, lt_ref, norm_ref, h_ref, v_out, w_out, h_out):
    v_out[...] = r_ref[...] / norm_ref[0:1]
    w_out[...] = jnp.transpose(lt_ref[...]) / norm_ref[1:2]
    h_out[...] = h_ref[...]


def local(tile_values, slot_codes, right_start, left_start, node_diagonal, row_scale):
    nr, nc = lax.axis_size("row"), lax.axis_size("col")
    slot_total, tile = tile_values.shape[:2]
    rows, ports = right_start.shape
    order = rows * nr * nc
    nz, ny = nr // 4, nc // 2
    vmem = pl.BlockSpec(memory_space=pltpu.VMEM)
    any_space = pl.BlockSpec(memory_space=pl.ANY)
    sem = pltpu.SemaphoreType.DMA
    scale_row = row_scale[None, :]

    gather_sems = [sem, sem, sem, sem((2 * (nz - 1),)), sem, sem((2,)), sem, sem, sem, sem]

    codes = jnp.pad(slot_codes.reshape(nr, 1, 2 * nc), ((0, 0), (0, 7), (0, 128 - 2 * nc)))
    vg, wg, got = pl.pallas_call(
        functools.partial(gather_kernel, nr, nc),
        out_shape=(
            jax.ShapeDtypeStruct((nr * rows, ports), BF16),
            jax.ShapeDtypeStruct((nc, ports, rows), BF16),
            jax.ShapeDtypeStruct((nc, nr, 8, 128), jnp.int32),
        ),
        in_specs=[vmem] * 4,
        out_specs=(vmem,) * 3,
        scratch_shapes=[pltpu.VMEM((nr, 8, 128), jnp.int32)] + gather_sems + [sem] * 4,
        compiler_params=pltpu.CompilerParams(
            collective_id=0, has_side_effects=True, vmem_limit_bytes=16 * 2**20
        ),
        cost_estimate=pl.CostEstimate(flops=10**10, bytes_accessed=10**7, transcendentals=0),
        name="gather",
    )(codes, right_start, left_start, scale_row)

    tile_values, got = lax.optimization_barrier((tile_values, got))
    got_tiles = lax.all_to_all(tile_values, ("row", "col"), split_axis=0, concat_axis=0, tiled=True)

    got = lax.dynamic_slice_in_dim(got[:, :, 0, :], 2 * lax.axis_index("col"), 2, axis=2)
    got_codes = jnp.transpose(got, (1, 0, 2)).reshape(slot_total)
    places = 4 * nr * nc
    hit = got_codes[None, :] == jnp.arange(places, dtype=jnp.int32)[:, None]
    slots = jnp.max(jnp.where(hit, jnp.arange(slot_total, dtype=jnp.int32)[None, :], -1), axis=1)
    slots = jnp.where(slots < 0, slot_total, slots)

    h_rows = ports // nc
    right_rest, left_rest, norms, projections = pl.pallas_call(
        functools.partial(krylov_kernel, nr, nc, order),
        out_shape=(
            jax.ShapeDtypeStruct((rows, ports), F32),
            jax.ShapeDtypeStruct((ports, rows), F32),
            jax.ShapeDtypeStruct((8, ports), F32),
            jax.ShapeDtypeStruct((ITERS, ports, ports), F32),
        ),
        in_specs=[pl.BlockSpec(memory_space=pltpu.SMEM)] + [any_space] * 3 + [vmem] * 6,
        out_specs=(vmem,) * 4,
        scratch_shapes=[
            pltpu.VMEM((slot_total + 1, tile, tile), BF16),
            pltpu.VMEM((2 * nc * tile, 2 * nr * tile), BF16),
            pltpu.VMEM((nr * rows, ports), BF16),
            pltpu.VMEM((nc, ports, rows), BF16),
            pltpu.VMEM((rows, ports), F32),
            pltpu.VMEM((ports, rows), F32),
            pltpu.VMEM((nc - 1, rows, ports), BF16),
            pltpu.VMEM((nc - 1, rows, ports), BF16),
            pltpu.VMEM((2 * nz, ports, rows), F32),
            pltpu.VMEM((2 * nz, ports, rows), F32),
            pltpu.VMEM((2 * (nz - 1), ports, rows), BF16),
            pltpu.VMEM((2 * (nz - 1), ports, rows), BF16),
            pltpu.VMEM((2, ports, rows), F32),
            pltpu.VMEM((ports, rows), F32),
            pltpu.VMEM((ports, rows), F32),
            pltpu.VMEM((ports, ports), F32),
            pltpu.VMEM((h_rows, ports), F32),
            pltpu.VMEM((nr, h_rows, ports), F32),
            pltpu.VMEM((nc, h_rows, ports), F32),
            pltpu.VMEM((ports, ports), F32),
            pltpu.VMEM((8, ports), F32),
            pltpu.VMEM((8, ports), F32),
            pltpu.VMEM((nr, 8, ports), F32),
            pltpu.VMEM((nc, 8, ports), F32),
        ]
        + [sem] * 3
        + gather_sems
        + [sem, sem((nc - 1,)), sem, sem((2 * nz,)), sem, sem((2,))]
        + [sem] * 12,
        compiler_params=pltpu.CompilerParams(
            collective_id=1, has_side_effects=True, vmem_limit_bytes=58 * 2**20
        ),
        name="krylov",
    )(
        slots, got_tiles, vg, wg, right_start, left_start,
        node_diagonal[:, None], node_diagonal[None, :], row_scale[:, None], scale_row,
    )
    return tuple(
        pl.pallas_call(
            finish_kernel,
            out_shape=(
                jax.ShapeDtypeStruct((rows, ports), F32),
                jax.ShapeDtypeStruct((rows, ports), F32),
                jax.ShapeDtypeStruct((ITERS, ports, ports), F32),
            ),
            in_specs=[vmem] * 4,
            out_specs=(vmem,) * 3,
            name="finish",
        )(right_rest, left_rest, norms, projections)
    )


def solution(mesh):
    return jax.shard_map(
        local,
        mesh=mesh,
        in_specs=(
            P(("row", "col"), None, None),
            P(("row", "col")),
            P(("row", "col"), None),
            P(("row", "col"), None),
            P(("row", "col")),
            P(("row", "col")),
        ),
        out_specs=(P(("row", "col"), None), P(("row", "col"), None), P()),
        check_vma=False,
    )
```

```python
import functools

import jax
import jax.numpy as jnp
from jax import lax
from jax.experimental import pallas as pl
from jax.experimental.pallas import tpu as pltpu
from jax.sharding import PartitionSpec as P

ITERS = 2
epsilon = 1e-06
MESH = pl.DeviceIdType.MESH
F32 = jnp.float32
BF16 = jnp.bfloat16
HIGHEST = lax.Precision.HIGHEST


def span(index, size):
    return pl.ds(pl.multiple_of(index * size, size), size)


def each(low, high, body):
    def step(i, carry):
        body(i)
        return carry

    lax.fori_loop(low, high, step, 0)


def remote(src, dst, send, recv, to):
    return pltpu.make_async_remote_copy(
        src_ref=src, dst_ref=dst, send_sem=send, recv_sem=recv, device_id=to, device_id_type=MESH
    )


class Place:
    def __init__(self, nr, nc):
        self.nr, self.nc, self.nz, self.ny = nr, nc, nr // 4, nc // 2
        self.row, self.col = lax.axis_index("row"), lax.axis_index("col")
        self.z, self.xl, self.core = self.row // 4, (self.row // 2) % 2, self.row % 2
        self.xh, self.y = self.col // self.ny, self.col % self.ny

    def row_at(self, d):
        return lax.rem(self.row + d + self.nr, self.nr)

    def col_at(self, d):
        return lax.rem(self.col + d + self.nc, self.nc)

    def z_at(self, d):
        return lax.rem(self.z + d + self.nz, self.nz)

    def y_at(self, d):
        return lax.rem(self.y + d + self.ny, self.ny)

    def row_of(self, z, xl, core):
        return z * 4 + xl * 2 + core

    def col_of(self, xh, y):
        return xh * self.ny + y

    def greet(self):
        barrier = pltpu.get_barrier_semaphore()
        each(1, self.nr, lambda d: pl.semaphore_signal(
            barrier, inc=1, device_id=(self.row_at(d), self.col), device_id_type=MESH))
        each(1, self.nc, lambda d: pl.semaphore_signal(
            barrier, inc=1, device_id=(self.row, self.col_at(d)), device_id_type=MESH))
        return lambda: pl.semaphore_wait(barrier, self.nr + self.nc - 2)


class RightGather:
    def __init__(self, me, vg, block, sems):
        self.me, self.vg, self.block = me, vg, block
        self.x_ss, self.x_rs, self.z_ss, self.z_rs, self.f_ss, self.f_rs = sems

    def slot(self, r):
        return self.vg.at[span(r, self.block)]

    def x_copy(self, r):
        me = self.me
        return remote(self.slot(r), self.slot(r), self.x_ss, self.x_rs, (me.row_of(me.z, 1 - me.xl, me.core), me.col))

    def z_copy(self, second, d, r):
        me = self.me
        i = second * (me.nz - 1) + d - 1
        to = (me.row_of(me.z_at(d), me.xl, me.core), me.col)
        return remote(self.slot(r), self.slot(r), self.z_ss, self.z_rs.at[i], to)

    def f_copy(self, second, r, blocks=0):
        me = self.me
        at = self.vg.at[pl.ds(0, blocks * self.block)] if blocks else self.slot(r)
        return remote(at, at, self.f_ss, self.f_rs.at[second], (me.row_of(me.z, me.xl, 1 - me.core), me.col))

    def from_z(self, second, d):
        me = self.me
        return me.row_of(me.z_at(-d), 1 - me.xl if second else me.xl, me.core)

    def start(self):
        me = self.me
        self.x_copy(me.row).start()
        each(1, me.nz, lambda d: self.z_copy(0, d, me.row).start())
        self.f_copy(0, me.row).start()

    def pass_x(self):
        r = self.from_z(1, 0)
        self.x_copy(r).wait_recv()
        each(1, self.me.nz, lambda d: self.z_copy(1, d, r).start())
        self.f_copy(1, r).start()

    def pass_z(self, second):
        def one(d):
            r = self.from_z(second, d)
            self.z_copy(second, d, r).wait_recv()
            self.f_copy(second, r).start()

        each(1, self.me.nz, one)

    def arrive(self, second):
        self.f_copy(second, 0, self.me.nz).wait_recv()

    def sent(self):
        me = self.me
        self.x_copy(me.row).wait_send()
        at = self.vg.at[pl.ds(0, 2 * (me.nz - 1) * self.block)]
        remote(at, at, self.z_ss, self.x_rs, (me.row_of(me.z, 1 - me.xl, me.core), me.col)).wait_send()
        self.f_copy(0, 0, 2 * me.nz).wait_send()


class LeftGather:
    def __init__(self, me, wg, sems):
        self.me, self.wg = me, wg
        self.x_ss, self.x_rs, self.y_ss, self.y_rs = sems

    def x_copy(self, c):
        me = self.me
        return remote(self.wg.at[c], self.wg.at[c], self.x_ss, self.x_rs, (me.row, me.col_of(1 - me.xh, me.y)))

    def y_copy(self, d, c):
        me = self.me
        to = (me.row, me.col_of(me.xh, me.y_at(d)))
        return remote(self.wg.at[c], self.wg.at[c], self.y_ss, self.y_rs, to)

    def y_all(self):
        me = self.me
        at = self.wg.at[pl.ds(0, 2 * (me.ny - 1))]
        return remote(at, at, self.y_ss, self.y_rs, (me.row, me.col_of(1 - me.xh, me.y)))

    def start(self):
        me = self.me
        self.x_copy(me.col).start()
        each(1, me.ny, lambda d: self.y_copy(d, me.col).start())

    def pass_x(self):
        me = self.me
        c = me.col_of(1 - me.xh, me.y)
        self.x_copy(c).wait_recv()
        each(1, me.ny, lambda d: self.y_copy(d, c).start())

    def arrive(self):
        self.y_all().wait_recv()

    def sent(self):
        self.x_copy(self.me.col).wait_send()
        self.y_all().wait_send()


class Exchange:
    def __init__(self, me, along_row, src, slots, ss, rs, pick=None):
        self.me, self.along_row, self.src, self.slots, self.ss, self.rs = me, along_row, src, slots, ss, rs
        self.pick = pick or (lambda i: src)
        self.size = me.nr if along_row else me.nc
        self.mine = me.row if along_row else me.col

    def at(self, d):
        return self.me.row_at(d) if self.along_row else self.me.col_at(d)

    def copy(self, d, slot):
        me = self.me
        to = (self.at(d), me.col) if self.along_row else (me.row, self.at(d))
        return remote(self.pick(self.at(d)), self.slots.at[slot], self.ss, self.rs, to)

    def start(self):
        each(1, self.size, lambda d: self.copy(d, self.mine).start())

    def all(self):
        me = self.me
        at = self.slots.at[pl.ds(0, self.size - 1)]
        to = (self.at(1), me.col) if self.along_row else (me.row, self.at(1))
        return remote(at, at, self.ss, self.rs, to)

    def total(self):
        self.all().wait_recv()
        total = self.slots[0]
        for i in range(1, self.size):
            total += self.slots[i]
        return total

    def sent(self):
        self.all().wait_send()


def codes_kernel(nr, nc, codes, got, got_row, c1_ss, c1_rs, c2_ss, c2_rs):
    me = Place(nr, nc)
    hold = me.greet()
    got_row[me.row] = codes[me.row]

    def c1_copy(d, slot):
        return remote(codes.at[me.row_at(d)], got_row.at[slot], c1_ss, c1_rs, (me.row_at(d), me.col))

    def c2_copy(d, slot):
        return remote(got_row, got.at[slot], c2_ss, c2_rs, (me.row, me.col_at(d)))

    def c1_all():
        at = got_row.at[pl.ds(0, nr - 1)]
        return remote(at, at, c1_ss, c1_rs, (me.row_at(1), me.col))

    def c2_all():
        at = got.at[pl.ds(0, nc - 1)]
        return remote(at, at, c2_ss, c2_rs, (me.row, me.col_at(1)))

    hold()
    each(1, nr, lambda d: c1_copy(d, me.row).start())
    c1_all().wait_recv()
    each(1, nc, lambda d: c2_copy(d, me.col).start())
    got[me.col] = got_row[...]
    c2_all().wait_recv()
    c1_all().wait_send()
    c2_all().wait_send()


def krylov_kernel(
    nr, nc, order,
    slots_ref, tiles_hbm, right_ref, left_ref, diag_col, diag_row, scale_col, scale_row,
    r_new, lt_new, norm_out, h_out,
    tiles, ta, vg, wg, v_ref, wt,
    r_send, r_recv, sib_send, sib_recv, l_send, l_recv, l_keep, x_send, x_recv,
    h_loc, h_part, h_from_row, h_from_col, h_full,
    n_loc, n_part, n_from_row, n_from_col,
    tile_sem, *sems,
):
    me = Place(nr, nc)
    row, col, nz = me.row, me.col, me.nz
    tile = tiles.shape[1]
    block = 2 * tile
    slot_total = tiles_hbm.shape[0]
    h_rows = h_loc.shape[0] // nc
    v = RightGather(me, vg, block, sems[:6])
    w = LeftGather(me, wg, sems[6:10])
    (r_ss, r_rs, s_ss, s_rs, l_ss, l_rs, x_ss, x_rs, h1_ss, h1_rs, h2_ss, h2_rs, h3_ss, h3_rs,
     n1_ss, n1_rs, n2_ss, n2_rs) = sems[10:]

    def r_copy(d):
        return remote(r_send.at[d - 1], r_recv.at[d - 1], r_ss, r_rs.at[d - 1], (row, me.col_at(d)))

    def r_sent():
        remote(r_send, r_recv, r_ss, r_rs.at[0], (row, me.col_at(1))).wait_send()

    def s_copy(e):
        to = (me.row_of(me.z, me.xl, 1 - me.core), col)
        return remote(sib_send.at[e], sib_recv.at[e], s_ss, s_rs.at[e], to)

    def s_sent():
        remote(sib_send, sib_recv, s_ss, s_rs.at[0], (me.row_of(me.z, me.xl, 1 - me.core), col)).wait_send()

    def l_copy(i):
        to = (me.row_of(me.z_at(i % (nz - 1) + 1), me.xl, me.core), col)
        return remote(l_send.at[i], l_recv.at[i], l_ss, l_rs.at[i // (nz - 1)], to)

    def l_sent():
        remote(l_send, l_recv, l_ss, l_rs.at[0], (me.row_of(me.z, 1 - me.xl, me.core), col)).wait_send()

    def l_arrive(home):
        at = l_recv.at[pl.ds(home * (nz - 1), nz - 1)]
        remote(at, at, l_ss, l_rs.at[home], (me.row_of(me.z, 1 - me.xl, me.core), col)).wait_recv()

    def x_copy():
        return remote(x_send, x_recv, x_ss, x_rs, (me.row_of(me.z, 1 - me.xl, me.core), col))

    def h3_copy(d, slot):
        at = h_full.at[span(slot, h_rows)]
        return remote(at, at, h3_ss, h3_rs, (row, me.col_at(d)))

    def h3_all():
        at = h_full.at[pl.ds(0, (nc - 1) * h_rows)]
        return remote(at, at, h3_ss, h3_rs, (row, me.col_at(1)))

    h1 = Exchange(me, False, h_loc, h_from_col, h1_ss, h1_rs, lambda i: h_loc.at[span(i, h_rows)])
    h2 = Exchange(me, True, h_part, h_from_row, h2_ss, h2_rs)
    n1 = Exchange(me, True, n_loc, n_from_row, n1_ss, n1_rs)
    n2 = Exchange(me, False, n_part, n_from_col, n2_ss, n2_rs)

    load = pltpu.make_async_copy(tiles_hbm, tiles.at[pl.ds(0, slot_total)], tile_sem)
    load.start()
    hold = me.greet()
    v_ref[...] = right_ref[...]
    vg[span(row, block)] = right_ref[...].astype(BF16)
    w_first = jnp.transpose(right_ref[...] + left_ref[...])
    wt[...] = w_first
    wg[col] = (scale_row[...] * w_first).astype(BF16)
    hold()
    v.start()
    w.start()
    n_loc[...] = jnp.zeros_like(n_loc)
    tiles[slot_total] = jnp.zeros((tile, tile), BF16)
    load.wait()
    v.pass_x()

    def one_row(a):
        for b in range(2 * nr):
            ta[span(a, tile), b * tile : (b + 1) * tile] = tiles[slots_ref[a * 2 * nr + b]]

    each(0, 2 * nc, one_row)

    def right_half(c, xl):
        total = None
        for z in range(nz):
            at = span(2 * z + xl, 2 * block)
            part = jnp.dot(ta[span(c, block), at], vg[at], preferred_element_type=F32)
            total = part if total is None else total + part
        return total

    def drain():
        r_sent()
        s_sent()
        l_sent()
        x_copy().wait_send()
        h1.sent()
        h2.sent()
        h3_all().wait_send()
        n1.sent()
        n2.sent()

    def left_part(r):
        rows = jnp.concatenate([wg[c] for c in range(nc)], axis=1)
        return jnp.dot(rows, ta[:, span(r, block)], preferred_element_type=F32)

    def xl_of(home):
        return me.xl * home + (1 - me.xl) * (1 - home)

    def norm_of(total):
        return jnp.sqrt(total * (1.0 / order) + epsilon)

    for turn in range(ITERS):
        last = turn == ITERS - 1
        if turn:
            v.pass_x()
        v.pass_z(0)
        w.pass_x()
        if turn:
            drain()
        v.arrive(0)

        def right_first(d):
            sib_send[d] = right_half(me.col_at(d), me.xl)

        each(0, nc, right_first)
        v.pass_z(1)
        v.arrive(1)

        def right_step(d):
            r_send[d - 1] = (sib_send[d] + right_half(me.col_at(d), 1 - me.xl)).astype(BF16)
            r_copy(d).start()

        each(1, nc, right_step)
        r_new[...] = sib_send[0] + right_half(col, 1 - me.xl) + diag_col[...] * v_ref[...]

        w.arrive()

        def left_other(e):
            sib_send[e] = left_part(me.row_of(me.z_at(e % nz + 1), xl_of(e // nz), 1 - me.core))
            s_copy(e).start()

        def left_own(e):
            s_copy(e).wait_recv()
            return left_part(me.row_of(me.z_at(e % nz + 1), xl_of(e // nz), me.core)) + sib_recv[e]

        for home in range(2):
            each(home * nz, home * nz + nz, left_other)

            def left_away(d, home=home):
                i = home * (nz - 1) + d
                l_send[i] = left_own(home * nz + d).astype(BF16)
                l_copy(i).start()

            each(0, nz - 1, left_away)
            l_keep[home] = left_own(home * nz + nz - 1)

        def right_sum(d):
            r_copy(d).wait_recv()
            r_new[...] += r_recv[d - 1].astype(F32)

        each(1, nc, right_sum)
        r_new[...] = scale_col[...] * r_new[...]

        h_loc[...] = jnp.dot(wt[...], r_new[...], precision=HIGHEST, preferred_element_type=F32)
        h1.start()
        h_from_col[col] = h_loc[span(col, h_rows)]

        def left_sum(home):
            l_arrive(home)
            total = l_keep[home]
            for d in range(nz - 1):
                total += l_recv[home * (nz - 1) + d].astype(F32)
            return total

        x_send[...] = left_sum(0)
        x_copy().start()
        part = h1.total()
        h_part[...] = part
        h2.start()
        h_from_row[row] = part
        v.sent()
        w.sent()

        h_full[span(col, h_rows)] = h2.total() * (1.0 / order)
        each(1, nc, lambda d: h3_copy(d, col).start())
        scaled = scale_row[...] * wt[...]
        lt_new[...] = left_sum(1) + diag_row[...] * scaled
        h3_all().wait_recv()

        project = h_full[...]
        rest = r_new[...] - jnp.dot(v_ref[...], project, precision=HIGHEST, preferred_element_type=F32)
        r_new[...] = rest
        n_loc[0:1] = jnp.sum(rest * rest, axis=0, keepdims=True)

        h_out[turn] = h_full[...]
        lt_new[...] -= jnp.dot(h_full[...], wt[...], precision=HIGHEST, preferred_element_type=F32)
        x_copy().wait_recv()
        lt_new[...] += x_recv[...]
        left_rest = lt_new[...]
        n_loc[1:2] = jnp.sum(jnp.transpose(left_rest * left_rest), axis=0, keepdims=True)
        n1.start()
        n_from_row[row] = n_loc[...]
        n_part[...] = n1.total()
        n2.start()
        n_from_col[col] = n_part[...]

        total = n2.total()
        if last:
            drain()
        norms = norm_of(total)
        if last:
            norm_out[...] = norms
        else:
            v_new = r_new[...] / norms[0:1]
            v_ref[...] = v_new
            vg[span(row, block)] = v_new.astype(BF16)
            v.start()
            size = lt_new.shape
            w_new = lt_new[...] / jnp.transpose(jnp.broadcast_to(norms[1:2], (size[1], size[0])))
            wt[...] = w_new
            wg[col] = (scale_row[...] * w_new).astype(BF16)
            w.start()


def finish_kernel(r_ref, lt_ref, norm_ref, h_ref, v_out, w_out, h_out):
    v_out[...] = r_ref[...] / norm_ref[0:1]
    w_out[...] = jnp.transpose(lt_ref[...]) / norm_ref[1:2]
    h_out[...] = h_ref[...]


def local(tile_values, slot_codes, right_start, left_start, node_diagonal, row_scale):
    nr, nc = lax.axis_size("row"), lax.axis_size("col")
    slot_total, tile = tile_values.shape[:2]
    rows, ports = right_start.shape
    order = rows * nr * nc
    nz, ny = nr // 4, nc // 2
    vmem = pl.BlockSpec(memory_space=pltpu.VMEM)
    any_space = pl.BlockSpec(memory_space=pl.ANY)
    sem = pltpu.SemaphoreType.DMA
    scale_row = row_scale[None, :]

    gather_sems = [sem, sem, sem, sem((2 * (nz - 1),)), sem, sem((2,)), sem, sem, sem, sem]

    got_tiles = lax.all_to_all(tile_values, ("row", "col"), split_axis=0, concat_axis=0, tiled=True)
    codes = jnp.pad(slot_codes.reshape(nr, 1, 2 * nc), ((0, 0), (0, 7), (0, 128 - 2 * nc)))
    got = pl.pallas_call(
        functools.partial(codes_kernel, nr, nc),
        out_shape=jax.ShapeDtypeStruct((nc, nr, 8, 128), jnp.int32),
        in_specs=[vmem],
        out_specs=vmem,
        scratch_shapes=[pltpu.VMEM((nr, 8, 128), jnp.int32)] + [sem] * 4,
        compiler_params=pltpu.CompilerParams(
            collective_id=0, has_side_effects=True, vmem_limit_bytes=16 * 2**20
        ),
        cost_estimate=pl.CostEstimate(flops=10**10, bytes_accessed=10**7, transcendentals=0),
        name="codes",
    )(codes)

    got = lax.dynamic_slice_in_dim(got[:, :, 0, :], 2 * lax.axis_index("col"), 2, axis=2)
    got_codes = jnp.transpose(got, (1, 0, 2)).reshape(slot_total)
    places = 4 * nr * nc
    hit = got_codes[None, :] == jnp.arange(places, dtype=jnp.int32)[:, None]
    slots = jnp.max(jnp.where(hit, jnp.arange(slot_total, dtype=jnp.int32)[None, :], -1), axis=1)
    slots = jnp.where(slots < 0, slot_total, slots)

    h_rows = ports // nc
    right_rest, left_rest, norms, projections = pl.pallas_call(
        functools.partial(krylov_kernel, nr, nc, order),
        out_shape=(
            jax.ShapeDtypeStruct((rows, ports), F32),
            jax.ShapeDtypeStruct((ports, rows), F32),
            jax.ShapeDtypeStruct((8, ports), F32),
            jax.ShapeDtypeStruct((ITERS, ports, ports), F32),
        ),
        in_specs=[pl.BlockSpec(memory_space=pltpu.SMEM)] + [any_space] + [vmem] * 6,
        out_specs=(vmem,) * 4,
        scratch_shapes=[
            pltpu.VMEM((slot_total + 1, tile, tile), BF16),
            pltpu.VMEM((2 * nc * tile, 2 * nr * tile), BF16),
            pltpu.VMEM((nr * rows, ports), BF16),
            pltpu.VMEM((nc, ports, rows), BF16),
            pltpu.VMEM((rows, ports), F32),
            pltpu.VMEM((ports, rows), F32),
            pltpu.VMEM((nc - 1, rows, ports), BF16),
            pltpu.VMEM((nc - 1, rows, ports), BF16),
            pltpu.VMEM((2 * nz, ports, rows), F32),
            pltpu.VMEM((2 * nz, ports, rows), F32),
            pltpu.VMEM((2 * (nz - 1), ports, rows), BF16),
            pltpu.VMEM((2 * (nz - 1), ports, rows), BF16),
            pltpu.VMEM((2, ports, rows), F32),
            pltpu.VMEM((ports, rows), F32),
            pltpu.VMEM((ports, rows), F32),
            pltpu.VMEM((ports, ports), F32),
            pltpu.VMEM((h_rows, ports), F32),
            pltpu.VMEM((nr, h_rows, ports), F32),
            pltpu.VMEM((nc, h_rows, ports), F32),
            pltpu.VMEM((ports, ports), F32),
            pltpu.VMEM((8, ports), F32),
            pltpu.VMEM((8, ports), F32),
            pltpu.VMEM((nr, 8, ports), F32),
            pltpu.VMEM((nc, 8, ports), F32),
        ]
        + [sem]
        + gather_sems
        + [sem, sem((nc - 1,)), sem, sem((2 * nz,)), sem, sem((2,))]
        + [sem] * 12,
        compiler_params=pltpu.CompilerParams(
            collective_id=1, has_side_effects=True, vmem_limit_bytes=58 * 2**20
        ),
        name="krylov",
    )(
        slots, got_tiles, right_start, left_start,
        node_diagonal[:, None], node_diagonal[None, :], row_scale[:, None], scale_row,
    )
    return tuple(
        pl.pallas_call(
            finish_kernel,
            out_shape=(
                jax.ShapeDtypeStruct((rows, ports), F32),
                jax.ShapeDtypeStruct((rows, ports), F32),
                jax.ShapeDtypeStruct((ITERS, ports, ports), F32),
            ),
            in_specs=[vmem] * 4,
            out_specs=(vmem,) * 3,
            name="finish",
        )(right_rest, left_rest, norms, projections)
    )


def solution(mesh):
    return jax.shard_map(
        local,
        mesh=mesh,
        in_specs=(
            P(("row", "col"), None, None),
            P(("row", "col")),
            P(("row", "col"), None),
            P(("row", "col"), None),
            P(("row", "col")),
            P(("row", "col")),
        ),
        out_specs=(P(("row", "col"), None), P(("row", "col"), None), P()),
        check_vma=False,
    )
```

```python
import functools

import jax
import jax.numpy as jnp
from jax import lax
from jax.experimental import pallas as pl
from jax.experimental.pallas import tpu as pltpu
from jax.sharding import PartitionSpec as P

ITERS = 2
epsilon = 1e-06
MESH = pl.DeviceIdType.MESH
F32 = jnp.float32
BF16 = jnp.bfloat16
HIGHEST = lax.Precision.HIGHEST


def span(index, size):
    return pl.ds(pl.multiple_of(index * size, size), size)


def each(low, high, body):
    def step(i, carry):
        body(i)
        return carry

    lax.fori_loop(low, high, step, 0)


def remote(src, dst, send, recv, to):
    return pltpu.make_async_remote_copy(
        src_ref=src, dst_ref=dst, send_sem=send, recv_sem=recv, device_id=to, device_id_type=MESH
    )


class Place:
    def __init__(self, nr, nc):
        self.nr, self.nc, self.nz, self.ny = nr, nc, nr // 4, nc // 2
        self.row, self.col = lax.axis_index("row"), lax.axis_index("col")
        self.z, self.xl, self.core = self.row // 4, (self.row // 2) % 2, self.row % 2
        self.xh, self.y = self.col // self.ny, self.col % self.ny

    def row_at(self, d):
        return lax.rem(self.row + d + self.nr, self.nr)

    def col_at(self, d):
        return lax.rem(self.col + d + self.nc, self.nc)

    def z_at(self, d):
        return lax.rem(self.z + d + self.nz, self.nz)

    def y_at(self, d):
        return lax.rem(self.y + d + self.ny, self.ny)

    def row_of(self, z, xl, core):
        return z * 4 + xl * 2 + core

    def col_of(self, xh, y):
        return xh * self.ny + y

    def greet(self):
        barrier = pltpu.get_barrier_semaphore()
        each(1, self.nr, lambda d: pl.semaphore_signal(
            barrier, inc=1, device_id=(self.row_at(d), self.col), device_id_type=MESH))
        each(1, self.nc, lambda d: pl.semaphore_signal(
            barrier, inc=1, device_id=(self.row, self.col_at(d)), device_id_type=MESH))
        return lambda: pl.semaphore_wait(barrier, self.nr + self.nc - 2)


class RightGather:
    def __init__(self, me, vg, block, sems):
        self.me, self.vg, self.block = me, vg, block
        self.x_ss, self.x_rs, self.z_ss, self.z_rs, self.f_ss, self.f_rs = sems

    def slot(self, r):
        return self.vg.at[span(r, self.block)]

    def x_copy(self, r):
        me = self.me
        return remote(self.slot(r), self.slot(r), self.x_ss, self.x_rs, (me.row_of(me.z, 1 - me.xl, me.core), me.col))

    def z_copy(self, second, d, r):
        me = self.me
        i = second * (me.nz - 1) + d - 1
        to = (me.row_of(me.z_at(d), me.xl, me.core), me.col)
        return remote(self.slot(r), self.slot(r), self.z_ss, self.z_rs.at[i], to)

    def f_copy(self, second, r, blocks=0):
        me = self.me
        at = self.vg.at[pl.ds(0, blocks * self.block)] if blocks else self.slot(r)
        return remote(at, at, self.f_ss, self.f_rs.at[second], (me.row_of(me.z, me.xl, 1 - me.core), me.col))

    def from_z(self, second, d):
        me = self.me
        return me.row_of(me.z_at(-d), 1 - me.xl if second else me.xl, me.core)

    def start(self):
        me = self.me
        self.x_copy(me.row).start()
        each(1, me.nz, lambda d: self.z_copy(0, d, me.row).start())
        self.f_copy(0, me.row).start()

    def pass_x(self):
        r = self.from_z(1, 0)
        self.x_copy(r).wait_recv()
        each(1, self.me.nz, lambda d: self.z_copy(1, d, r).start())
        self.f_copy(1, r).start()

    def pass_z(self, second):
        def one(d):
            r = self.from_z(second, d)
            self.z_copy(second, d, r).wait_recv()
            self.f_copy(second, r).start()

        each(1, self.me.nz, one)

    def arrive(self, second):
        self.f_copy(second, 0, self.me.nz).wait_recv()

    def sent(self):
        me = self.me
        self.x_copy(me.row).wait_send()
        at = self.vg.at[pl.ds(0, 2 * (me.nz - 1) * self.block)]
        remote(at, at, self.z_ss, self.x_rs, (me.row_of(me.z, 1 - me.xl, me.core), me.col)).wait_send()
        self.f_copy(0, 0, 2 * me.nz).wait_send()


class LeftGather:
    def __init__(self, me, wg, sems):
        self.me, self.wg = me, wg
        self.x_ss, self.x_rs, self.y_ss, self.y_rs = sems

    def x_copy(self, c):
        me = self.me
        return remote(self.wg.at[c], self.wg.at[c], self.x_ss, self.x_rs, (me.row, me.col_of(1 - me.xh, me.y)))

    def y_copy(self, d, c):
        me = self.me
        to = (me.row, me.col_of(me.xh, me.y_at(d)))
        return remote(self.wg.at[c], self.wg.at[c], self.y_ss, self.y_rs, to)

    def y_all(self):
        me = self.me
        at = self.wg.at[pl.ds(0, 2 * (me.ny - 1))]
        return remote(at, at, self.y_ss, self.y_rs, (me.row, me.col_of(1 - me.xh, me.y)))

    def start(self):
        me = self.me
        self.x_copy(me.col).start()
        each(1, me.ny, lambda d: self.y_copy(d, me.col).start())

    def pass_x(self):
        me = self.me
        c = me.col_of(1 - me.xh, me.y)
        self.x_copy(c).wait_recv()
        each(1, me.ny, lambda d: self.y_copy(d, c).start())

    def arrive(self):
        self.y_all().wait_recv()

    def sent(self):
        self.x_copy(self.me.col).wait_send()
        self.y_all().wait_send()


class Exchange:
    def __init__(self, me, along_row, src, slots, ss, rs, pick=None):
        self.me, self.along_row, self.src, self.slots, self.ss, self.rs = me, along_row, src, slots, ss, rs
        self.pick = pick or (lambda i: src)
        self.size = me.nr if along_row else me.nc
        self.mine = me.row if along_row else me.col

    def at(self, d):
        return self.me.row_at(d) if self.along_row else self.me.col_at(d)

    def copy(self, d, slot):
        me = self.me
        to = (self.at(d), me.col) if self.along_row else (me.row, self.at(d))
        return remote(self.pick(self.at(d)), self.slots.at[slot], self.ss, self.rs, to)

    def start(self):
        each(1, self.size, lambda d: self.copy(d, self.mine).start())

    def all(self):
        me = self.me
        at = self.slots.at[pl.ds(0, self.size - 1)]
        to = (self.at(1), me.col) if self.along_row else (me.row, self.at(1))
        return remote(at, at, self.ss, self.rs, to)

    def total(self):
        self.all().wait_recv()
        total = self.slots[0]
        for i in range(1, self.size):
            total += self.slots[i]
        return total

    def sent(self):
        self.all().wait_send()


def codes_kernel(nr, nc, codes, got, got_row, c1_ss, c1_rs, c2_ss, c2_rs):
    me = Place(nr, nc)
    hold = me.greet()
    got_row[me.row] = codes[me.row]

    def c1_copy(d, slot):
        return remote(codes.at[me.row_at(d)], got_row.at[slot], c1_ss, c1_rs, (me.row_at(d), me.col))

    def c2_copy(d, slot):
        return remote(got_row, got.at[slot], c2_ss, c2_rs, (me.row, me.col_at(d)))

    def c1_all():
        at = got_row.at[pl.ds(0, nr - 1)]
        return remote(at, at, c1_ss, c1_rs, (me.row_at(1), me.col))

    def c2_all():
        at = got.at[pl.ds(0, nc - 1)]
        return remote(at, at, c2_ss, c2_rs, (me.row, me.col_at(1)))

    hold()
    each(1, nr, lambda d: c1_copy(d, me.row).start())
    c1_all().wait_recv()
    each(1, nc, lambda d: c2_copy(d, me.col).start())
    got[me.col] = got_row[...]
    c2_all().wait_recv()
    c1_all().wait_send()
    c2_all().wait_send()


def krylov_kernel(
    nr, nc, order,
    slots_ref, tiles_hbm, right_ref, left_ref, diag_col, diag_row, scale_col, scale_row,
    r_new, lt_new, norm_out, h_out,
    tiles, ta, vg, wg, v_ref, wt,
    r_send, r_recv, sib_send, sib_recv, l_send, l_recv, l_keep, x_send, x_recv,
    h_loc, h_part, h_from_row, h_from_col, h_full,
    n_loc, n_part, n_from_row, n_from_col,
    tile_sem, *sems,
):
    me = Place(nr, nc)
    row, col, nz = me.row, me.col, me.nz
    tile = tiles.shape[1]
    block = 2 * tile
    slot_total = tiles_hbm.shape[0]
    h_rows = h_loc.shape[0] // nc
    v = RightGather(me, vg, block, sems[:6])
    w = LeftGather(me, wg, sems[6:10])
    (r_ss, r_rs, s_ss, s_rs, l_ss, l_rs, x_ss, x_rs, h1_ss, h1_rs, h2_ss, h2_rs, h3_ss, h3_rs,
     n1_ss, n1_rs, n2_ss, n2_rs) = sems[10:]

    def r_copy(d):
        return remote(r_send.at[d - 1], r_recv.at[d - 1], r_ss, r_rs.at[d - 1], (row, me.col_at(d)))

    def r_sent():
        remote(r_send, r_recv, r_ss, r_rs.at[0], (row, me.col_at(1))).wait_send()

    def s_copy(e):
        to = (me.row_of(me.z, me.xl, 1 - me.core), col)
        return remote(sib_send.at[e], sib_recv.at[e], s_ss, s_rs.at[e], to)

    def s_sent():
        remote(sib_send, sib_recv, s_ss, s_rs.at[0], (me.row_of(me.z, me.xl, 1 - me.core), col)).wait_send()

    def l_copy(i):
        to = (me.row_of(me.z_at(i % (nz - 1) + 1), me.xl, me.core), col)
        return remote(l_send.at[i], l_recv.at[i], l_ss, l_rs.at[i // (nz - 1)], to)

    def l_sent():
        remote(l_send, l_recv, l_ss, l_rs.at[0], (me.row_of(me.z, 1 - me.xl, me.core), col)).wait_send()

    def l_arrive(home):
        at = l_recv.at[pl.ds(home * (nz - 1), nz - 1)]
        remote(at, at, l_ss, l_rs.at[home], (me.row_of(me.z, 1 - me.xl, me.core), col)).wait_recv()

    def x_copy():
        return remote(x_send, x_recv, x_ss, x_rs, (me.row_of(me.z, 1 - me.xl, me.core), col))

    def h3_copy(d, slot):
        at = h_full.at[span(slot, h_rows)]
        return remote(at, at, h3_ss, h3_rs, (row, me.col_at(d)))

    def h3_all():
        at = h_full.at[pl.ds(0, (nc - 1) * h_rows)]
        return remote(at, at, h3_ss, h3_rs, (row, me.col_at(1)))

    h1 = Exchange(me, False, h_loc, h_from_col, h1_ss, h1_rs, lambda i: h_loc.at[span(i, h_rows)])
    h2 = Exchange(me, True, h_part, h_from_row, h2_ss, h2_rs)
    n1 = Exchange(me, True, n_loc, n_from_row, n1_ss, n1_rs)
    n2 = Exchange(me, False, n_part, n_from_col, n2_ss, n2_rs)

    load = pltpu.make_async_copy(tiles_hbm, tiles.at[pl.ds(0, slot_total)], tile_sem)
    load.start()
    hold = me.greet()
    v_ref[...] = right_ref[...]
    vg[span(row, block)] = right_ref[...].astype(BF16)
    w_first = jnp.transpose(right_ref[...] + left_ref[...])
    wt[...] = w_first
    wg[col] = (scale_row[...] * w_first).astype(BF16)
    hold()
    v.start()
    w.start()
    n_loc[...] = jnp.zeros_like(n_loc)
    tiles[slot_total] = jnp.zeros((tile, tile), BF16)
    load.wait()
    v.pass_x()

    def one_row(a):
        for b in range(2 * nr):
            ta[span(a, tile), b * tile : (b + 1) * tile] = tiles[slots_ref[a * 2 * nr + b]]

    each(0, 2 * nc, one_row)

    def right_half(c, xl):
        total = None
        for z in range(nz):
            at = span(2 * z + xl, 2 * block)
            part = jnp.dot(ta[span(c, block), at], vg[at], preferred_element_type=F32)
            total = part if total is None else total + part
        return total

    def drain():
        r_sent()
        s_sent()
        l_sent()
        x_copy().wait_send()
        h1.sent()
        h2.sent()
        h3_all().wait_send()
        n1.sent()
        n2.sent()

    def left_part(r):
        rows = jnp.concatenate([wg[c] for c in range(nc)], axis=1)
        return jnp.dot(rows, ta[:, span(r, block)], preferred_element_type=F32)

    def xl_of(home):
        return me.xl * home + (1 - me.xl) * (1 - home)

    def norm_of(total):
        return jnp.sqrt(total * (1.0 / order) + epsilon)

    for turn in range(ITERS):
        last = turn == ITERS - 1
        if turn:
            v.pass_x()
        v.pass_z(0)
        w.pass_x()
        if turn:
            drain()
        v.arrive(0)

        def right_first(d):
            sib_send[d] = right_half(me.col_at(d), me.xl)

        each(0, nc, right_first)
        v.pass_z(1)
        v.arrive(1)

        def right_step(d):
            r_send[d - 1] = (sib_send[d] + right_half(me.col_at(d), 1 - me.xl)).astype(BF16)
            r_copy(d).start()

        each(1, nc, right_step)
        r_new[...] = sib_send[0] + right_half(col, 1 - me.xl) + diag_col[...] * v_ref[...]

        w.arrive()

        def left_other(e):
            sib_send[e] = left_part(me.row_of(me.z_at(e % nz + 1), xl_of(e // nz), 1 - me.core))
            s_copy(e).start()

        def left_own(e):
            s_copy(e).wait_recv()
            return left_part(me.row_of(me.z_at(e % nz + 1), xl_of(e // nz), me.core)) + sib_recv[e]

        for home in range(2):
            each(home * nz, home * nz + nz, left_other)

            def left_away(d, home=home):
                i = home * (nz - 1) + d
                l_send[i] = left_own(home * nz + d).astype(BF16)
                l_copy(i).start()

            each(0, nz - 1, left_away)
            l_keep[home] = left_own(home * nz + nz - 1)

        def right_sum(d):
            r_copy(d).wait_recv()
            r_new[...] += r_recv[d - 1].astype(F32)

        each(1, nc, right_sum)
        r_new[...] = scale_col[...] * r_new[...]

        h_loc[...] = jnp.dot(wt[...], r_new[...], precision=HIGHEST, preferred_element_type=F32)
        h1.start()
        h_from_col[col] = h_loc[span(col, h_rows)]

        def left_sum(home):
            l_arrive(home)
            total = l_keep[home]
            for d in range(nz - 1):
                total += l_recv[home * (nz - 1) + d].astype(F32)
            return total

        x_send[...] = left_sum(0)
        x_copy().start()
        part = h1.total()
        h_part[...] = part
        h2.start()
        h_from_row[row] = part
        v.sent()
        w.sent()

        h_full[span(col, h_rows)] = h2.total() * (1.0 / order)
        each(1, nc, lambda d: h3_copy(d, col).start())
        scaled = scale_row[...] * wt[...]
        lt_new[...] = left_sum(1) + diag_row[...] * scaled
        h3_all().wait_recv()

        project = h_full[...]
        rest = r_new[...] - jnp.dot(v_ref[...], project, precision=HIGHEST, preferred_element_type=F32)
        r_new[...] = rest
        n_loc[0:1] = jnp.sum(rest * rest, axis=0, keepdims=True)

        h_out[turn] = h_full[...]
        lt_new[...] -= jnp.dot(h_full[...], wt[...], precision=HIGHEST, preferred_element_type=F32)
        x_copy().wait_recv()
        lt_new[...] += x_recv[...]
        left_rest = lt_new[...]
        n_loc[1:2] = jnp.sum(jnp.transpose(left_rest * left_rest), axis=0, keepdims=True)
        n1.start()
        n_from_row[row] = n_loc[...]
        n_part[...] = n1.total()
        n2.start()
        n_from_col[col] = n_part[...]

        total = n2.total()
        if last:
            drain()
        norms = norm_of(total)
        if last:
            norm_out[...] = norms
        else:
            v_new = r_new[...] / norms[0:1]
            v_ref[...] = v_new
            vg[span(row, block)] = v_new.astype(BF16)
            v.start()
            size = lt_new.shape
            w_new = lt_new[...] / jnp.transpose(jnp.broadcast_to(norms[1:2], (size[1], size[0])))
            wt[...] = w_new
            wg[col] = (scale_row[...] * w_new).astype(BF16)
            w.start()


def finish_kernel(r_ref, lt_ref, norm_ref, h_ref, v_out, w_out, h_out):
    v_out[...] = r_ref[...] / norm_ref[0:1]
    w_out[...] = jnp.transpose(lt_ref[...]) / norm_ref[1:2]
    h_out[...] = h_ref[...]


def local(tile_values, slot_codes, right_start, left_start, node_diagonal, row_scale):
    nr, nc = lax.axis_size("row"), lax.axis_size("col")
    slot_total, tile = tile_values.shape[:2]
    rows, ports = right_start.shape
    order = rows * nr * nc
    nz, ny = nr // 4, nc // 2
    vmem = pl.BlockSpec(memory_space=pltpu.VMEM)
    any_space = pl.BlockSpec(memory_space=pl.ANY)
    sem = pltpu.SemaphoreType.DMA
    scale_row = row_scale[None, :]

    gather_sems = [sem, sem, sem, sem((2 * (nz - 1),)), sem, sem((2,)), sem, sem, sem, sem]

    codes = jnp.pad(slot_codes.reshape(nr, 1, 2 * nc), ((0, 0), (0, 7), (0, 128 - 2 * nc)))
    got = pl.pallas_call(
        functools.partial(codes_kernel, nr, nc),
        out_shape=jax.ShapeDtypeStruct((nc, nr, 8, 128), jnp.int32),
        in_specs=[vmem],
        out_specs=vmem,
        scratch_shapes=[pltpu.VMEM((nr, 8, 128), jnp.int32)] + [sem] * 4,
        compiler_params=pltpu.CompilerParams(
            collective_id=0, has_side_effects=True, vmem_limit_bytes=16 * 2**20
        ),
        cost_estimate=pl.CostEstimate(flops=10**10, bytes_accessed=10**7, transcendentals=0),
        name="codes",
    )(codes)

    tile_values, got = lax.optimization_barrier((tile_values, got))
    got_tiles = lax.all_to_all(tile_values, ("row", "col"), split_axis=0, concat_axis=0, tiled=True)

    got = lax.dynamic_slice_in_dim(got[:, :, 0, :], 2 * lax.axis_index("col"), 2, axis=2)
    got_codes = jnp.transpose(got, (1, 0, 2)).reshape(slot_total)
    places = 4 * nr * nc
    hit = got_codes[None, :] == jnp.arange(places, dtype=jnp.int32)[:, None]
    slots = jnp.max(jnp.where(hit, jnp.arange(slot_total, dtype=jnp.int32)[None, :], -1), axis=1)
    slots = jnp.where(slots < 0, slot_total, slots)

    h_rows = ports // nc
    right_rest, left_rest, norms, projections = pl.pallas_call(
        functools.partial(krylov_kernel, nr, nc, order),
        out_shape=(
            jax.ShapeDtypeStruct((rows, ports), F32),
            jax.ShapeDtypeStruct((ports, rows), F32),
            jax.ShapeDtypeStruct((8, ports), F32),
            jax.ShapeDtypeStruct((ITERS, ports, ports), F32),
        ),
        in_specs=[pl.BlockSpec(memory_space=pltpu.SMEM)] + [any_space] + [vmem] * 6,
        out_specs=(vmem,) * 4,
        scratch_shapes=[
            pltpu.VMEM((slot_total + 1, tile, tile), BF16),
            pltpu.VMEM((2 * nc * tile, 2 * nr * tile), BF16),
            pltpu.VMEM((nr * rows, ports), BF16),
            pltpu.VMEM((nc, ports, rows), BF16),
            pltpu.VMEM((rows, ports), F32),
            pltpu.VMEM((ports, rows), F32),
            pltpu.VMEM((nc - 1, rows, ports), BF16),
            pltpu.VMEM((nc - 1, rows, ports), BF16),
            pltpu.VMEM((2 * nz, ports, rows), F32),
            pltpu.VMEM((2 * nz, ports, rows), F32),
            pltpu.VMEM((2 * (nz - 1), ports, rows), BF16),
            pltpu.VMEM((2 * (nz - 1), ports, rows), BF16),
            pltpu.VMEM((2, ports, rows), F32),
            pltpu.VMEM((ports, rows), F32),
            pltpu.VMEM((ports, rows), F32),
            pltpu.VMEM((ports, ports), F32),
            pltpu.VMEM((h_rows, ports), F32),
            pltpu.VMEM((nr, h_rows, ports), F32),
            pltpu.VMEM((nc, h_rows, ports), F32),
            pltpu.VMEM((ports, ports), F32),
            pltpu.VMEM((8, ports), F32),
            pltpu.VMEM((8, ports), F32),
            pltpu.VMEM((nr, 8, ports), F32),
            pltpu.VMEM((nc, 8, ports), F32),
        ]
        + [sem]
        + gather_sems
        + [sem, sem((nc - 1,)), sem, sem((2 * nz,)), sem, sem((2,))]
        + [sem] * 12,
        compiler_params=pltpu.CompilerParams(
            collective_id=1, has_side_effects=True, vmem_limit_bytes=58 * 2**20
        ),
        name="krylov",
    )(
        slots, got_tiles, right_start, left_start,
        node_diagonal[:, None], node_diagonal[None, :], row_scale[:, None], scale_row,
    )
    return tuple(
        pl.pallas_call(
            finish_kernel,
            out_shape=(
                jax.ShapeDtypeStruct((rows, ports), F32),
                jax.ShapeDtypeStruct((rows, ports), F32),
                jax.ShapeDtypeStruct((ITERS, ports, ports), F32),
            ),
            in_specs=[vmem] * 4,
            out_specs=(vmem,) * 3,
            name="finish",
        )(right_rest, left_rest, norms, projections)
    )


def solution(mesh):
    return jax.shard_map(
        local,
        mesh=mesh,
        in_specs=(
            P(("row", "col"), None, None),
            P(("row", "col")),
            P(("row", "col"), None),
            P(("row", "col"), None),
            P(("row", "col")),
            P(("row", "col")),
        ),
        out_specs=(P(("row", "col"), None), P(("row", "col"), None), P()),
        check_vma=False,
    )
```

```python
import functools

import jax
import jax.numpy as jnp
from jax import lax
from jax.experimental import pallas as pl
from jax.experimental.pallas import tpu as pltpu
from jax.sharding import PartitionSpec as P

ITERS = 2
epsilon = 1e-06
MESH = pl.DeviceIdType.MESH
F32 = jnp.float32
BF16 = jnp.bfloat16
HIGHEST = lax.Precision.HIGHEST


def span(index, size):
    return pl.ds(pl.multiple_of(index * size, size), size)


def each(low, high, body):
    def step(i, carry):
        body(i)
        return carry

    lax.fori_loop(low, high, step, 0)


def remote(src, dst, send, recv, to):
    return pltpu.make_async_remote_copy(
        src_ref=src, dst_ref=dst, send_sem=send, recv_sem=recv, device_id=to, device_id_type=MESH
    )


class Place:
    def __init__(self, nr, nc):
        self.nr, self.nc, self.nz, self.ny = nr, nc, nr // 4, nc // 2
        self.row, self.col = lax.axis_index("row"), lax.axis_index("col")
        self.z, self.xl, self.core = self.row // 4, (self.row // 2) % 2, self.row % 2
        self.xh, self.y = self.col // self.ny, self.col % self.ny

    def row_at(self, d):
        return lax.rem(self.row + d + self.nr, self.nr)

    def col_at(self, d):
        return lax.rem(self.col + d + self.nc, self.nc)

    def z_at(self, d):
        return lax.rem(self.z + d + self.nz, self.nz)

    def y_at(self, d):
        return lax.rem(self.y + d + self.ny, self.ny)

    def row_of(self, z, xl, core):
        return z * 4 + xl * 2 + core

    def col_of(self, xh, y):
        return xh * self.ny + y

    def greet(self):
        barrier = pltpu.get_barrier_semaphore()
        each(1, self.nr, lambda d: pl.semaphore_signal(
            barrier, inc=1, device_id=(self.row_at(d), self.col), device_id_type=MESH))
        each(1, self.nc, lambda d: pl.semaphore_signal(
            barrier, inc=1, device_id=(self.row, self.col_at(d)), device_id_type=MESH))
        return lambda: pl.semaphore_wait(barrier, self.nr + self.nc - 2)


class RightGather:
    def __init__(self, me, vg, block, sems):
        self.me, self.vg, self.block = me, vg, block
        self.x_ss, self.x_rs, self.z_ss, self.z_rs, self.f_ss, self.f_rs = sems

    def slot(self, r):
        return self.vg.at[span(r, self.block)]

    def x_copy(self, r):
        me = self.me
        return remote(self.slot(r), self.slot(r), self.x_ss, self.x_rs, (me.row_of(me.z, 1 - me.xl, me.core), me.col))

    def z_copy(self, second, d, r):
        me = self.me
        i = second * (me.nz - 1) + d - 1
        to = (me.row_of(me.z_at(d), me.xl, me.core), me.col)
        return remote(self.slot(r), self.slot(r), self.z_ss, self.z_rs.at[i], to)

    def f_copy(self, second, r, blocks=0):
        me = self.me
        at = self.vg.at[pl.ds(0, blocks * self.block)] if blocks else self.slot(r)
        return remote(at, at, self.f_ss, self.f_rs.at[second], (me.row_of(me.z, me.xl, 1 - me.core), me.col))

    def from_z(self, second, d):
        me = self.me
        return me.row_of(me.z_at(-d), 1 - me.xl if second else me.xl, me.core)

    def start(self):
        me = self.me
        self.x_copy(me.row).start()
        each(1, me.nz, lambda d: self.z_copy(0, d, me.row).start())
        self.f_copy(0, me.row).start()

    def pass_x(self):
        r = self.from_z(1, 0)
        self.x_copy(r).wait_recv()
        each(1, self.me.nz, lambda d: self.z_copy(1, d, r).start())
        self.f_copy(1, r).start()

    def pass_z(self, second):
        def one(d):
            r = self.from_z(second, d)
            self.z_copy(second, d, r).wait_recv()
            self.f_copy(second, r).start()

        each(1, self.me.nz, one)

    def arrive(self, second):
        self.f_copy(second, 0, self.me.nz).wait_recv()

    def sent(self):
        me = self.me
        self.x_copy(me.row).wait_send()
        at = self.vg.at[pl.ds(0, 2 * (me.nz - 1) * self.block)]
        remote(at, at, self.z_ss, self.x_rs, (me.row_of(me.z, 1 - me.xl, me.core), me.col)).wait_send()
        self.f_copy(0, 0, 2 * me.nz).wait_send()


class LeftGather:
    def __init__(self, me, wg, sems):
        self.me, self.wg = me, wg
        self.x_ss, self.x_rs, self.y_ss, self.y_rs = sems

    def x_copy(self, c):
        me = self.me
        return remote(self.wg.at[c], self.wg.at[c], self.x_ss, self.x_rs, (me.row, me.col_of(1 - me.xh, me.y)))

    def y_copy(self, d, c):
        me = self.me
        to = (me.row, me.col_of(me.xh, me.y_at(d)))
        return remote(self.wg.at[c], self.wg.at[c], self.y_ss, self.y_rs, to)

    def y_all(self):
        me = self.me
        at = self.wg.at[pl.ds(0, 2 * (me.ny - 1))]
        return remote(at, at, self.y_ss, self.y_rs, (me.row, me.col_of(1 - me.xh, me.y)))

    def start(self):
        me = self.me
        self.x_copy(me.col).start()
        each(1, me.ny, lambda d: self.y_copy(d, me.col).start())

    def pass_x(self):
        me = self.me
        c = me.col_of(1 - me.xh, me.y)
        self.x_copy(c).wait_recv()
        each(1, me.ny, lambda d: self.y_copy(d, c).start())

    def arrive(self):
        self.y_all().wait_recv()

    def sent(self):
        self.x_copy(self.me.col).wait_send()
        self.y_all().wait_send()


class Exchange:
    def __init__(self, me, along_row, src, slots, ss, rs, pick=None):
        self.me, self.along_row, self.src, self.slots, self.ss, self.rs = me, along_row, src, slots, ss, rs
        self.pick = pick or (lambda i: src)
        self.size = me.nr if along_row else me.nc
        self.mine = me.row if along_row else me.col

    def at(self, d):
        return self.me.row_at(d) if self.along_row else self.me.col_at(d)

    def copy(self, d, slot):
        me = self.me
        to = (self.at(d), me.col) if self.along_row else (me.row, self.at(d))
        return remote(self.pick(self.at(d)), self.slots.at[slot], self.ss, self.rs, to)

    def start(self):
        each(1, self.size, lambda d: self.copy(d, self.mine).start())

    def all(self):
        me = self.me
        at = self.slots.at[pl.ds(0, self.size - 1)]
        to = (self.at(1), me.col) if self.along_row else (me.row, self.at(1))
        return remote(at, at, self.ss, self.rs, to)

    def total(self):
        self.all().wait_recv()
        total = self.slots[0]
        for i in range(1, self.size):
            total += self.slots[i]
        return total

    def sent(self):
        self.all().wait_send()


def codes_kernel(nr, nc, codes, got, got_row, c1_ss, c1_rs, c2_ss, c2_rs):
    me = Place(nr, nc)
    hold = me.greet()
    got_row[me.row] = codes[me.row]

    def c1_copy(d, slot):
        return remote(codes.at[me.row_at(d)], got_row.at[slot], c1_ss, c1_rs, (me.row_at(d), me.col))

    def c2_copy(d, slot):
        return remote(got_row, got.at[slot], c2_ss, c2_rs, (me.row, me.col_at(d)))

    def c1_all():
        at = got_row.at[pl.ds(0, nr - 1)]
        return remote(at, at, c1_ss, c1_rs, (me.row_at(1), me.col))

    def c2_all():
        at = got.at[pl.ds(0, nc - 1)]
        return remote(at, at, c2_ss, c2_rs, (me.row, me.col_at(1)))

    hold()
    each(1, nr, lambda d: c1_copy(d, me.row).start())
    c1_all().wait_recv()
    each(1, nc, lambda d: c2_copy(d, me.col).start())
    got[me.col] = got_row[...]
    c2_all().wait_recv()
    c1_all().wait_send()
    c2_all().wait_send()


def krylov_kernel(
    nr, nc, order,
    slots_ref, tiles_hbm, right_ref, left_ref, diag_col, diag_row, scale_col, scale_row,
    r_new, lt_new, norm_out, h_out,
    tiles, ta, vg, wg, v_ref, wt,
    r_send, r_recv, sib_send, sib_recv, l_send, l_recv, l_keep, x_send, x_recv,
    h_loc, h_part, h_from_row, h_from_col, h_full,
    n_loc, n_part, n_from_row, n_from_col,
    tile_sem, *sems,
):
    me = Place(nr, nc)
    row, col, nz = me.row, me.col, me.nz
    tile = tiles.shape[1]
    block = 2 * tile
    slot_total = tiles_hbm.shape[0]
    h_rows = h_loc.shape[0] // nc
    v = RightGather(me, vg, block, sems[:6])
    w = LeftGather(me, wg, sems[6:10])
    (r_ss, r_rs, s_ss, s_rs, l_ss, l_rs, x_ss, x_rs, h1_ss, h1_rs, h2_ss, h2_rs, h3_ss, h3_rs,
     n1_ss, n1_rs, n2_ss, n2_rs) = sems[10:]

    def r_copy(d):
        return remote(r_send.at[d - 1], r_recv.at[d - 1], r_ss, r_rs.at[d - 1], (row, me.col_at(d)))

    def r_sent():
        remote(r_send, r_recv, r_ss, r_rs.at[0], (row, me.col_at(1))).wait_send()

    def s_copy(e):
        to = (me.row_of(me.z, me.xl, 1 - me.core), col)
        return remote(sib_send.at[e], sib_recv.at[e], s_ss, s_rs.at[e], to)

    def s_sent():
        remote(sib_send, sib_recv, s_ss, s_rs.at[0], (me.row_of(me.z, me.xl, 1 - me.core), col)).wait_send()

    def l_copy(i):
        to = (me.row_of(me.z_at(i % (nz - 1) + 1), me.xl, me.core), col)
        return remote(l_send.at[i], l_recv.at[i], l_ss, l_rs.at[i // (nz - 1)], to)

    def l_sent():
        remote(l_send, l_recv, l_ss, l_rs.at[0], (me.row_of(me.z, 1 - me.xl, me.core), col)).wait_send()

    def l_arrive(home):
        at = l_recv.at[pl.ds(home * (nz - 1), nz - 1)]
        remote(at, at, l_ss, l_rs.at[home], (me.row_of(me.z, 1 - me.xl, me.core), col)).wait_recv()

    def x_copy():
        return remote(x_send, x_recv, x_ss, x_rs, (me.row_of(me.z, 1 - me.xl, me.core), col))

    def h3_copy(d, slot):
        at = h_full.at[span(slot, h_rows)]
        return remote(at, at, h3_ss, h3_rs, (row, me.col_at(d)))

    def h3_all():
        at = h_full.at[pl.ds(0, (nc - 1) * h_rows)]
        return remote(at, at, h3_ss, h3_rs, (row, me.col_at(1)))

    h1 = Exchange(me, False, h_loc, h_from_col, h1_ss, h1_rs, lambda i: h_loc.at[span(i, h_rows)])
    h2 = Exchange(me, True, h_part, h_from_row, h2_ss, h2_rs)
    n1 = Exchange(me, True, n_loc, n_from_row, n1_ss, n1_rs)
    n2 = Exchange(me, False, n_part, n_from_col, n2_ss, n2_rs)

    load = pltpu.make_async_copy(tiles_hbm, tiles.at[pl.ds(0, slot_total)], tile_sem)
    load.start()
    hold = me.greet()
    v_ref[...] = right_ref[...]
    vg[span(row, block)] = right_ref[...].astype(BF16)
    w_first = jnp.transpose(right_ref[...] + left_ref[...])
    wt[...] = w_first
    wg[col] = (scale_row[...] * w_first).astype(BF16)
    hold()
    v.start()
    w.start()
    n_loc[...] = jnp.zeros_like(n_loc)
    tiles[slot_total] = jnp.zeros((tile, tile), BF16)
    load.wait()
    v.pass_x()

    def one_row(a):
        for b in range(2 * nr):
            ta[span(a, tile), b * tile : (b + 1) * tile] = tiles[slots_ref[a * 2 * nr + b]]

    each(0, 2 * nc, one_row)

    def right_half(c, xl):
        total = None
        for z in range(nz):
            at = span(2 * z + xl, 2 * block)
            part = jnp.dot(ta[span(c, block), at], vg[at], preferred_element_type=F32)
            total = part if total is None else total + part
        return total

    def drain():
        r_sent()
        s_sent()
        l_sent()
        x_copy().wait_send()
        h1.sent()
        h2.sent()
        h3_all().wait_send()
        n1.sent()
        n2.sent()

    def left_part(r):
        rows = jnp.concatenate([wg[c] for c in range(nc)], axis=1)
        return jnp.dot(rows, ta[:, span(r, block)], preferred_element_type=F32)

    def xl_of(home):
        return me.xl * home + (1 - me.xl) * (1 - home)

    def norm_of(total):
        return jnp.sqrt(total * (1.0 / order) + epsilon)

    for turn in range(ITERS):
        last = turn == ITERS - 1
        if turn:
            v.pass_x()
        v.pass_z(0)
        w.pass_x()
        if turn:
            drain()
        v.arrive(0)

        def right_first(d):
            sib_send[d] = right_half(me.col_at(d), me.xl)

        each(0, nc, right_first)
        v.pass_z(1)
        v.arrive(1)

        def right_step(d):
            r_send[d - 1] = (sib_send[d] + right_half(me.col_at(d), 1 - me.xl)).astype(BF16)
            r_copy(d).start()

        each(1, nc, right_step)
        r_new[...] = sib_send[0] + right_half(col, 1 - me.xl) + diag_col[...] * v_ref[...]

        w.arrive()

        def left_other(e):
            sib_send[e] = left_part(me.row_of(me.z_at(e % nz + 1), xl_of(e // nz), 1 - me.core))
            s_copy(e).start()

        def left_own(e):
            s_copy(e).wait_recv()
            return left_part(me.row_of(me.z_at(e % nz + 1), xl_of(e // nz), me.core)) + sib_recv[e]

        for home in range(2):
            each(home * nz, home * nz + nz, left_other)

            def left_away(d, home=home):
                i = home * (nz - 1) + d
                l_send[i] = left_own(home * nz + d).astype(BF16)
                l_copy(i).start()

            each(0, nz - 1, left_away)
            l_keep[home] = left_own(home * nz + nz - 1)

        def right_sum(d):
            r_copy(d).wait_recv()
            r_new[...] += r_recv[d - 1].astype(F32)

        each(1, nc, right_sum)
        r_new[...] = scale_col[...] * r_new[...]

        h_loc[...] = jnp.dot(wt[...], r_new[...], precision=HIGHEST, preferred_element_type=F32)
        h1.start()
        h_from_col[col] = h_loc[span(col, h_rows)]

        def left_sum(home):
            l_arrive(home)
            total = l_keep[home]
            for d in range(nz - 1):
                total += l_recv[home * (nz - 1) + d].astype(F32)
            return total

        x_send[...] = left_sum(0)
        x_copy().start()
        part = h1.total()
        h_part[...] = part
        h2.start()
        h_from_row[row] = part
        v.sent()
        w.sent()

        h_full[span(col, h_rows)] = h2.total() * (1.0 / order)
        each(1, nc, lambda d: h3_copy(d, col).start())
        scaled = scale_row[...] * wt[...]
        lt_new[...] = left_sum(1) + diag_row[...] * scaled
        h3_all().wait_recv()

        project = h_full[...]
        rest = r_new[...] - jnp.dot(v_ref[...], project, precision=HIGHEST, preferred_element_type=F32)
        r_new[...] = rest
        n_loc[0:1] = jnp.sum(rest * rest, axis=0, keepdims=True)

        h_out[turn] = h_full[...]
        lt_new[...] -= jnp.dot(h_full[...], wt[...], precision=HIGHEST, preferred_element_type=F32)
        x_copy().wait_recv()
        lt_new[...] += x_recv[...]
        left_rest = lt_new[...]
        n_loc[1:2] = jnp.sum(jnp.transpose(left_rest * left_rest), axis=0, keepdims=True)
        n1.start()
        n_from_row[row] = n_loc[...]
        n_part[...] = n1.total()
        n2.start()
        n_from_col[col] = n_part[...]

        total = n2.total()
        if last:
            drain()
        norms = norm_of(total)
        if last:
            norm_out[...] = norms
        else:
            v_new = r_new[...] / norms[0:1]
            v_ref[...] = v_new
            vg[span(row, block)] = v_new.astype(BF16)
            v.start()
            size = lt_new.shape
            w_new = lt_new[...] / jnp.transpose(jnp.broadcast_to(norms[1:2], (size[1], size[0])))
            wt[...] = w_new
            wg[col] = (scale_row[...] * w_new).astype(BF16)
            w.start()


def finish_kernel(r_ref, lt_ref, norm_ref, h_ref, v_out, w_out, h_out):
    v_out[...] = r_ref[...] / norm_ref[0:1]
    w_out[...] = jnp.transpose(lt_ref[...]) / norm_ref[1:2]
    h_out[...] = h_ref[...]


def local(tile_values, slot_codes, right_start, left_start, node_diagonal, row_scale):
    nr, nc = lax.axis_size("row"), lax.axis_size("col")
    slot_total, tile = tile_values.shape[:2]
    rows, ports = right_start.shape
    order = rows * nr * nc
    nz, ny = nr // 4, nc // 2
    vmem = pl.BlockSpec(memory_space=pltpu.VMEM)
    any_space = pl.BlockSpec(memory_space=pl.ANY)
    sem = pltpu.SemaphoreType.DMA
    scale_row = row_scale[None, :]

    gather_sems = [sem, sem, sem, sem((2 * (nz - 1),)), sem, sem((2,)), sem, sem, sem, sem]

    got_tiles = lax.all_to_all(tile_values, ("row", "col"), split_axis=0, concat_axis=0, tiled=True)
    codes = jnp.pad(slot_codes.reshape(nr, 1, 2 * nc), ((0, 0), (0, 0), (0, 128 - 2 * nc)))
    got = pl.pallas_call(
        functools.partial(codes_kernel, nr, nc),
        out_shape=jax.ShapeDtypeStruct((nc, nr, 1, 128), jnp.int32),
        in_specs=[vmem],
        out_specs=vmem,
        scratch_shapes=[pltpu.VMEM((nr, 1, 128), jnp.int32)] + [sem] * 4,
        compiler_params=pltpu.CompilerParams(
            collective_id=0, has_side_effects=True, vmem_limit_bytes=16 * 2**20
        ),
        cost_estimate=pl.CostEstimate(flops=10**10, bytes_accessed=10**7, transcendentals=0),
        name="codes",
    )(codes)

    got = lax.dynamic_slice_in_dim(got[:, :, 0, :], 2 * lax.axis_index("col"), 2, axis=2)
    got_codes = jnp.transpose(got, (1, 0, 2)).reshape(slot_total)
    places = 4 * nr * nc
    hit = got_codes[None, :] == jnp.arange(places, dtype=jnp.int32)[:, None]
    slots = jnp.max(jnp.where(hit, jnp.arange(slot_total, dtype=jnp.int32)[None, :], -1), axis=1)
    slots = jnp.where(slots < 0, slot_total, slots)

    h_rows = ports // nc
    right_rest, left_rest, norms, projections = pl.pallas_call(
        functools.partial(krylov_kernel, nr, nc, order),
        out_shape=(
            jax.ShapeDtypeStruct((rows, ports), F32),
            jax.ShapeDtypeStruct((ports, rows), F32),
            jax.ShapeDtypeStruct((8, ports), F32),
            jax.ShapeDtypeStruct((ITERS, ports, ports), F32),
        ),
        in_specs=[pl.BlockSpec(memory_space=pltpu.SMEM)] + [any_space] + [vmem] * 6,
        out_specs=(vmem,) * 4,
        scratch_shapes=[
            pltpu.VMEM((slot_total + 1, tile, tile), BF16),
            pltpu.VMEM((2 * nc * tile, 2 * nr * tile), BF16),
            pltpu.VMEM((nr * rows, ports), BF16),
            pltpu.VMEM((nc, ports, rows), BF16),
            pltpu.VMEM((rows, ports), F32),
            pltpu.VMEM((ports, rows), F32),
            pltpu.VMEM((nc - 1, rows, ports), BF16),
            pltpu.VMEM((nc - 1, rows, ports), BF16),
            pltpu.VMEM((2 * nz, ports, rows), F32),
            pltpu.VMEM((2 * nz, ports, rows), F32),
            pltpu.VMEM((2 * (nz - 1), ports, rows), BF16),
            pltpu.VMEM((2 * (nz - 1), ports, rows), BF16),
            pltpu.VMEM((2, ports, rows), F32),
            pltpu.VMEM((ports, rows), F32),
            pltpu.VMEM((ports, rows), F32),
            pltpu.VMEM((ports, ports), F32),
            pltpu.VMEM((h_rows, ports), F32),
            pltpu.VMEM((nr, h_rows, ports), F32),
            pltpu.VMEM((nc, h_rows, ports), F32),
            pltpu.VMEM((ports, ports), F32),
            pltpu.VMEM((8, ports), F32),
            pltpu.VMEM((8, ports), F32),
            pltpu.VMEM((nr, 8, ports), F32),
            pltpu.VMEM((nc, 8, ports), F32),
        ]
        + [sem]
        + gather_sems
        + [sem, sem((nc - 1,)), sem, sem((2 * nz,)), sem, sem((2,))]
        + [sem] * 12,
        compiler_params=pltpu.CompilerParams(
            collective_id=1, has_side_effects=True, vmem_limit_bytes=58 * 2**20
        ),
        name="krylov",
    )(
        slots, got_tiles, right_start, left_start,
        node_diagonal[:, None], node_diagonal[None, :], row_scale[:, None], scale_row,
    )
    return tuple(
        pl.pallas_call(
            finish_kernel,
            out_shape=(
                jax.ShapeDtypeStruct((rows, ports), F32),
                jax.ShapeDtypeStruct((rows, ports), F32),
                jax.ShapeDtypeStruct((ITERS, ports, ports), F32),
            ),
            in_specs=[vmem] * 4,
            out_specs=(vmem,) * 3,
            name="finish",
        )(right_rest, left_rest, norms, projections)
    )


def solution(mesh):
    return jax.shard_map(
        local,
        mesh=mesh,
        in_specs=(
            P(("row", "col"), None, None),
            P(("row", "col")),
            P(("row", "col"), None),
            P(("row", "col"), None),
            P(("row", "col")),
            P(("row", "col")),
        ),
        out_specs=(P(("row", "col"), None), P(("row", "col"), None), P()),
        check_vma=False,
    )
```

```python
import functools

import jax
import jax.numpy as jnp
from jax import lax
from jax.experimental import pallas as pl
from jax.experimental.pallas import tpu as pltpu
from jax.sharding import PartitionSpec as P

ITERS = 2
epsilon = 1e-06
MESH = pl.DeviceIdType.MESH
F32 = jnp.float32
BF16 = jnp.bfloat16
HIGHEST = lax.Precision.HIGHEST


def span(index, size):
    return pl.ds(pl.multiple_of(index * size, size), size)


def each(low, high, body):
    def step(i, carry):
        body(i)
        return carry

    lax.fori_loop(low, high, step, 0)


def remote(src, dst, send, recv, to):
    return pltpu.make_async_remote_copy(
        src_ref=src, dst_ref=dst, send_sem=send, recv_sem=recv, device_id=to, device_id_type=MESH
    )


class Place:
    def __init__(self, nr, nc):
        self.nr, self.nc, self.nz, self.ny = nr, nc, nr // 4, nc // 2
        self.row, self.col = lax.axis_index("row"), lax.axis_index("col")
        self.z, self.xl, self.core = self.row // 4, (self.row // 2) % 2, self.row % 2
        self.xh, self.y = self.col // self.ny, self.col % self.ny

    def row_at(self, d):
        return lax.rem(self.row + d + self.nr, self.nr)

    def col_at(self, d):
        return lax.rem(self.col + d + self.nc, self.nc)

    def z_at(self, d):
        return lax.rem(self.z + d + self.nz, self.nz)

    def y_at(self, d):
        return lax.rem(self.y + d + self.ny, self.ny)

    def row_of(self, z, xl, core):
        return z * 4 + xl * 2 + core

    def col_of(self, xh, y):
        return xh * self.ny + y

    def greet(self):
        barrier = pltpu.get_barrier_semaphore()
        each(1, self.nr, lambda d: pl.semaphore_signal(
            barrier, inc=1, device_id=(self.row_at(d), self.col), device_id_type=MESH))
        each(1, self.nc, lambda d: pl.semaphore_signal(
            barrier, inc=1, device_id=(self.row, self.col_at(d)), device_id_type=MESH))
        return lambda: pl.semaphore_wait(barrier, self.nr + self.nc - 2)


class RightGather:
    def __init__(self, me, vg, block, sems):
        self.me, self.vg, self.block = me, vg, block
        self.x_ss, self.x_rs, self.z_ss, self.z_rs, self.f_ss, self.f_rs = sems

    def slot(self, r):
        return self.vg.at[span(r, self.block)]

    def x_copy(self, r):
        me = self.me
        return remote(self.slot(r), self.slot(r), self.x_ss, self.x_rs, (me.row_of(me.z, 1 - me.xl, me.core), me.col))

    def z_copy(self, second, d, r):
        me = self.me
        i = second * (me.nz - 1) + d - 1
        to = (me.row_of(me.z_at(d), me.xl, me.core), me.col)
        return remote(self.slot(r), self.slot(r), self.z_ss, self.z_rs.at[i], to)

    def f_copy(self, second, r, blocks=0):
        me = self.me
        at = self.vg.at[pl.ds(0, blocks * self.block)] if blocks else self.slot(r)
        return remote(at, at, self.f_ss, self.f_rs.at[second], (me.row_of(me.z, me.xl, 1 - me.core), me.col))

    def from_z(self, second, d):
        me = self.me
        return me.row_of(me.z_at(-d), 1 - me.xl if second else me.xl, me.core)

    def start(self):
        me = self.me
        self.x_copy(me.row).start()
        each(1, me.nz, lambda d: self.z_copy(0, d, me.row).start())
        self.f_copy(0, me.row).start()

    def pass_x(self):
        r = self.from_z(1, 0)
        self.x_copy(r).wait_recv()
        each(1, self.me.nz, lambda d: self.z_copy(1, d, r).start())
        self.f_copy(1, r).start()

    def pass_z(self, second):
        def one(d):
            r = self.from_z(second, d)
            self.z_copy(second, d, r).wait_recv()
            self.f_copy(second, r).start()

        each(1, self.me.nz, one)

    def arrive(self, second):
        self.f_copy(second, 0, self.me.nz).wait_recv()

    def sent(self):
        me = self.me
        self.x_copy(me.row).wait_send()
        at = self.vg.at[pl.ds(0, 2 * (me.nz - 1) * self.block)]
        remote(at, at, self.z_ss, self.x_rs, (me.row_of(me.z, 1 - me.xl, me.core), me.col)).wait_send()
        self.f_copy(0, 0, 2 * me.nz).wait_send()


class LeftGather:
    def __init__(self, me, wg, sems):
        self.me, self.wg = me, wg
        self.x_ss, self.x_rs, self.y_ss, self.y_rs = sems

    def x_copy(self, c):
        me = self.me
        return remote(self.wg.at[c], self.wg.at[c], self.x_ss, self.x_rs, (me.row, me.col_of(1 - me.xh, me.y)))

    def y_copy(self, d, c):
        me = self.me
        to = (me.row, me.col_of(me.xh, me.y_at(d)))
        return remote(self.wg.at[c], self.wg.at[c], self.y_ss, self.y_rs, to)

    def y_all(self):
        me = self.me
        at = self.wg.at[pl.ds(0, 2 * (me.ny - 1))]
        return remote(at, at, self.y_ss, self.y_rs, (me.row, me.col_of(1 - me.xh, me.y)))

    def start(self):
        me = self.me
        self.x_copy(me.col).start()
        each(1, me.ny, lambda d: self.y_copy(d, me.col).start())

    def pass_x(self):
        me = self.me
        c = me.col_of(1 - me.xh, me.y)
        self.x_copy(c).wait_recv()
        each(1, me.ny, lambda d: self.y_copy(d, c).start())

    def arrive(self):
        self.y_all().wait_recv()

    def sent(self):
        self.x_copy(self.me.col).wait_send()
        self.y_all().wait_send()


class Exchange:
    def __init__(self, me, along_row, src, slots, ss, rs, pick=None):
        self.me, self.along_row, self.src, self.slots, self.ss, self.rs = me, along_row, src, slots, ss, rs
        self.pick = pick or (lambda i: src)
        self.size = me.nr if along_row else me.nc
        self.mine = me.row if along_row else me.col

    def at(self, d):
        return self.me.row_at(d) if self.along_row else self.me.col_at(d)

    def copy(self, d, slot):
        me = self.me
        to = (self.at(d), me.col) if self.along_row else (me.row, self.at(d))
        return remote(self.pick(self.at(d)), self.slots.at[slot], self.ss, self.rs, to)

    def start(self):
        each(1, self.size, lambda d: self.copy(d, self.mine).start())

    def all(self):
        me = self.me
        at = self.slots.at[pl.ds(0, self.size - 1)]
        to = (self.at(1), me.col) if self.along_row else (me.row, self.at(1))
        return remote(at, at, self.ss, self.rs, to)

    def total(self):
        self.all().wait_recv()
        total = self.slots[0]
        for i in range(1, self.size):
            total += self.slots[i]
        return total

    def sent(self):
        self.all().wait_send()


def codes_kernel(nr, nc, codes, got, got_row, c1_ss, c1_rs, c2_ss, c2_rs):
    me = Place(nr, nc)
    hold = me.greet()
    got_row[me.row] = codes[me.row]

    def c1_copy(d, slot):
        return remote(codes.at[me.row_at(d)], got_row.at[slot], c1_ss, c1_rs, (me.row_at(d), me.col))

    def c2_copy(d, slot):
        return remote(got_row, got.at[slot], c2_ss, c2_rs, (me.row, me.col_at(d)))

    def c1_all():
        at = got_row.at[pl.ds(0, nr - 1)]
        return remote(at, at, c1_ss, c1_rs, (me.row_at(1), me.col))

    def c2_all():
        at = got.at[pl.ds(0, nc - 1)]
        return remote(at, at, c2_ss, c2_rs, (me.row, me.col_at(1)))

    hold()
    each(1, nr, lambda d: c1_copy(d, me.row).start())
    c1_all().wait_recv()
    each(1, nc, lambda d: c2_copy(d, me.col).start())
    got[me.col] = got_row[...]
    c2_all().wait_recv()
    c1_all().wait_send()
    c2_all().wait_send()


def krylov_kernel(
    nr, nc, order,
    slots_ref, tiles_hbm, right_ref, left_ref, diag_col, diag_row, scale_col, scale_row,
    r_new, lt_new, norm_out, h_out,
    tiles, ta, vg, wg, v_ref, wt,
    r_send, r_recv, sib_send, sib_recv, l_send, l_recv, l_keep, x_send, x_recv,
    h_loc, h_part, h_from_row, h_from_col, h_full,
    n_loc, n_part, n_from_row, n_from_col,
    tile_sem, *sems,
):
    me = Place(nr, nc)
    row, col, nz = me.row, me.col, me.nz
    tile = tiles.shape[1]
    block = 2 * tile
    slot_total = tiles_hbm.shape[0]
    h_rows = h_loc.shape[0] // nc
    v = RightGather(me, vg, block, sems[:6])
    w = LeftGather(me, wg, sems[6:10])
    (r_ss, r_rs, s_ss, s_rs, l_ss, l_rs, x_ss, x_rs, h1_ss, h1_rs, h2_ss, h2_rs, h3_ss, h3_rs,
     n1_ss, n1_rs, n2_ss, n2_rs) = sems[10:]

    def right_to(d):
        across = (2 * me.ny - d) // me.ny
        xh = me.xh + across - 2 * me.xh * across
        return me.col_of(xh, me.y_at(d - me.ny + across * (me.ny - 1)))

    def r_copy(d):
        return remote(r_send.at[d - 1], r_recv.at[d - 1], r_ss, r_rs.at[d - 1], (row, right_to(d)))

    def r_sent():
        remote(r_send, r_recv, r_ss, r_rs.at[0], (row, me.col_at(1))).wait_send()

    def s_copy(e):
        to = (me.row_of(me.z, me.xl, 1 - me.core), col)
        return remote(sib_send.at[e], sib_recv.at[e], s_ss, s_rs.at[e], to)

    def s_sent():
        remote(sib_send, sib_recv, s_ss, s_rs.at[0], (me.row_of(me.z, me.xl, 1 - me.core), col)).wait_send()

    def l_copy(i):
        to = (me.row_of(me.z_at(i % (nz - 1) + 1), me.xl, me.core), col)
        return remote(l_send.at[i], l_recv.at[i], l_ss, l_rs.at[i // (nz - 1)], to)

    def l_sent():
        remote(l_send, l_recv, l_ss, l_rs.at[0], (me.row_of(me.z, 1 - me.xl, me.core), col)).wait_send()

    def l_arrive(home):
        at = l_recv.at[pl.ds(home * (nz - 1), nz - 1)]
        remote(at, at, l_ss, l_rs.at[home], (me.row_of(me.z, 1 - me.xl, me.core), col)).wait_recv()

    def x_copy():
        return remote(x_send, x_recv, x_ss, x_rs, (me.row_of(me.z, 1 - me.xl, me.core), col))

    def h3_copy(d, slot):
        at = h_full.at[span(slot, h_rows)]
        return remote(at, at, h3_ss, h3_rs, (row, me.col_at(d)))

    def h3_all():
        at = h_full.at[pl.ds(0, (nc - 1) * h_rows)]
        return remote(at, at, h3_ss, h3_rs, (row, me.col_at(1)))

    h1 = Exchange(me, False, h_loc, h_from_col, h1_ss, h1_rs, lambda i: h_loc.at[span(i, h_rows)])
    h2 = Exchange(me, True, h_part, h_from_row, h2_ss, h2_rs)
    n1 = Exchange(me, True, n_loc, n_from_row, n1_ss, n1_rs)
    n2 = Exchange(me, False, n_part, n_from_col, n2_ss, n2_rs)

    load = pltpu.make_async_copy(tiles_hbm, tiles.at[pl.ds(0, slot_total)], tile_sem)
    load.start()
    hold = me.greet()
    v_ref[...] = right_ref[...]
    vg[span(row, block)] = right_ref[...].astype(BF16)
    w_first = jnp.transpose(right_ref[...] + left_ref[...])
    wt[...] = w_first
    wg[col] = (scale_row[...] * w_first).astype(BF16)
    hold()
    v.start()
    w.start()
    n_loc[...] = jnp.zeros_like(n_loc)
    tiles[slot_total] = jnp.zeros((tile, tile), BF16)
    load.wait()
    v.pass_x()

    def one_row(a):
        for b in range(2 * nr):
            ta[span(a, tile), b * tile : (b + 1) * tile] = tiles[slots_ref[a * 2 * nr + b]]

    each(0, 2 * nc, one_row)

    def right_half(c, xl):
        total = None
        for z in range(nz):
            at = span(2 * z + xl, 2 * block)
            part = jnp.dot(ta[span(c, block), at], vg[at], preferred_element_type=F32)
            total = part if total is None else total + part
        return total

    def drain():
        r_sent()
        s_sent()
        l_sent()
        x_copy().wait_send()
        h1.sent()
        h2.sent()
        h3_all().wait_send()
        n1.sent()
        n2.sent()

    def left_part(r):
        rows = jnp.concatenate([wg[c] for c in range(nc)], axis=1)
        return jnp.dot(rows, ta[:, span(r, block)], preferred_element_type=F32)

    def xl_of(home):
        return me.xl * home + (1 - me.xl) * (1 - home)

    def norm_of(total):
        return jnp.sqrt(total * (1.0 / order) + epsilon)

    for turn in range(ITERS):
        last = turn == ITERS - 1
        if turn:
            v.pass_x()
        v.pass_z(0)
        w.pass_x()
        if turn:
            drain()
        v.arrive(0)

        def right_first(d):
            sib_send[d] = right_half(right_to(d), me.xl)

        each(1, nc, right_first)
        sib_send[0] = right_half(col, me.xl)
        v.pass_z(1)
        v.arrive(1)

        def right_step(d):
            r_send[d - 1] = (sib_send[d] + right_half(right_to(d), 1 - me.xl)).astype(BF16)
            r_copy(d).start()

        each(1, nc, right_step)
        r_new[...] = sib_send[0] + right_half(col, 1 - me.xl) + diag_col[...] * v_ref[...]

        w.arrive()

        def left_other(e):
            sib_send[e] = left_part(me.row_of(me.z_at(e % nz + 1), xl_of(e // nz), 1 - me.core))
            s_copy(e).start()

        def left_own(e):
            s_copy(e).wait_recv()
            return left_part(me.row_of(me.z_at(e % nz + 1), xl_of(e // nz), me.core)) + sib_recv[e]

        for home in range(2):
            each(home * nz, home * nz + nz, left_other)

            def left_away(d, home=home):
                i = home * (nz - 1) + d
                l_send[i] = left_own(home * nz + d).astype(BF16)
                l_copy(i).start()

            each(0, nz - 1, left_away)
            l_keep[home] = left_own(home * nz + nz - 1)

        def right_sum(d):
            r_copy(d).wait_recv()
            r_new[...] += r_recv[d - 1].astype(F32)

        each(1, nc, right_sum)
        r_new[...] = scale_col[...] * r_new[...]

        h_loc[...] = jnp.dot(wt[...], r_new[...], precision=HIGHEST, preferred_element_type=F32)
        h1.start()
        h_from_col[col] = h_loc[span(col, h_rows)]

        def left_sum(home):
            l_arrive(home)
            total = l_keep[home]
            for d in range(nz - 1):
                total += l_recv[home * (nz - 1) + d].astype(F32)
            return total

        x_send[...] = left_sum(0)
        x_copy().start()
        part = h1.total()
        h_part[...] = part
        h2.start()
        h_from_row[row] = part
        v.sent()
        w.sent()

        h_full[span(col, h_rows)] = h2.total() * (1.0 / order)
        each(1, nc, lambda d: h3_copy(d, col).start())
        scaled = scale_row[...] * wt[...]
        lt_new[...] = left_sum(1) + diag_row[...] * scaled
        h3_all().wait_recv()

        project = h_full[...]
        rest = r_new[...] - jnp.dot(v_ref[...], project, precision=HIGHEST, preferred_element_type=F32)
        r_new[...] = rest
        n_loc[0:1] = jnp.sum(rest * rest, axis=0, keepdims=True)

        h_out[turn] = h_full[...]
        lt_new[...] -= jnp.dot(h_full[...], wt[...], precision=HIGHEST, preferred_element_type=F32)
        x_copy().wait_recv()
        lt_new[...] += x_recv[...]
        left_rest = lt_new[...]
        n_loc[1:2] = jnp.sum(jnp.transpose(left_rest * left_rest), axis=0, keepdims=True)
        n1.start()
        n_from_row[row] = n_loc[...]
        n_part[...] = n1.total()
        n2.start()
        n_from_col[col] = n_part[...]

        total = n2.total()
        if last:
            drain()
        norms = norm_of(total)
        if last:
            norm_out[...] = norms
        else:
            v_new = r_new[...] / norms[0:1]
            v_ref[...] = v_new
            vg[span(row, block)] = v_new.astype(BF16)
            v.start()
            size = lt_new.shape
            w_new = lt_new[...] / jnp.transpose(jnp.broadcast_to(norms[1:2], (size[1], size[0])))
            wt[...] = w_new
            wg[col] = (scale_row[...] * w_new).astype(BF16)
            w.start()


def finish_kernel(r_ref, lt_ref, norm_ref, h_ref, v_out, w_out, h_out):
    v_out[...] = r_ref[...] / norm_ref[0:1]
    w_out[...] = jnp.transpose(lt_ref[...]) / norm_ref[1:2]
    h_out[...] = h_ref[...]


def local(tile_values, slot_codes, right_start, left_start, node_diagonal, row_scale):
    nr, nc = lax.axis_size("row"), lax.axis_size("col")
    slot_total, tile = tile_values.shape[:2]
    rows, ports = right_start.shape
    order = rows * nr * nc
    nz, ny = nr // 4, nc // 2
    vmem = pl.BlockSpec(memory_space=pltpu.VMEM)
    any_space = pl.BlockSpec(memory_space=pl.ANY)
    sem = pltpu.SemaphoreType.DMA
    scale_row = row_scale[None, :]

    gather_sems = [sem, sem, sem, sem((2 * (nz - 1),)), sem, sem((2,)), sem, sem, sem, sem]

    got_tiles = lax.all_to_all(tile_values, ("row", "col"), split_axis=0, concat_axis=0, tiled=True)
    codes = jnp.pad(slot_codes.reshape(nr, 1, 2 * nc), ((0, 0), (0, 0), (0, 128 - 2 * nc)))
    got = pl.pallas_call(
        functools.partial(codes_kernel, nr, nc),
        out_shape=jax.ShapeDtypeStruct((nc, nr, 1, 128), jnp.int32),
        in_specs=[vmem],
        out_specs=vmem,
        scratch_shapes=[pltpu.VMEM((nr, 1, 128), jnp.int32)] + [sem] * 4,
        compiler_params=pltpu.CompilerParams(
            collective_id=0, has_side_effects=True, vmem_limit_bytes=16 * 2**20
        ),
        cost_estimate=pl.CostEstimate(flops=10**10, bytes_accessed=10**7, transcendentals=0),
        name="codes",
    )(codes)

    got = lax.dynamic_slice_in_dim(got[:, :, 0, :], 2 * lax.axis_index("col"), 2, axis=2)
    got_codes = jnp.transpose(got, (1, 0, 2)).reshape(slot_total)
    places = 4 * nr * nc
    hit = got_codes[None, :] == jnp.arange(places, dtype=jnp.int32)[:, None]
    slots = jnp.max(jnp.where(hit, jnp.arange(slot_total, dtype=jnp.int32)[None, :], -1), axis=1)
    slots = jnp.where(slots < 0, slot_total, slots)

    h_rows = ports // nc
    right_rest, left_rest, norms, projections = pl.pallas_call(
        functools.partial(krylov_kernel, nr, nc, order),
        out_shape=(
            jax.ShapeDtypeStruct((rows, ports), F32),
            jax.ShapeDtypeStruct((ports, rows), F32),
            jax.ShapeDtypeStruct((8, ports), F32),
            jax.ShapeDtypeStruct((ITERS, ports, ports), F32),
        ),
        in_specs=[pl.BlockSpec(memory_space=pltpu.SMEM)] + [any_space] + [vmem] * 6,
        out_specs=(vmem,) * 4,
        scratch_shapes=[
            pltpu.VMEM((slot_total + 1, tile, tile), BF16),
            pltpu.VMEM((2 * nc * tile, 2 * nr * tile), BF16),
            pltpu.VMEM((nr * rows, ports), BF16),
            pltpu.VMEM((nc, ports, rows), BF16),
            pltpu.VMEM((rows, ports), F32),
            pltpu.VMEM((ports, rows), F32),
            pltpu.VMEM((nc - 1, rows, ports), BF16),
            pltpu.VMEM((nc - 1, rows, ports), BF16),
            pltpu.VMEM((2 * nz, ports, rows), F32),
            pltpu.VMEM((2 * nz, ports, rows), F32),
            pltpu.VMEM((2 * (nz - 1), ports, rows), BF16),
            pltpu.VMEM((2 * (nz - 1), ports, rows), BF16),
            pltpu.VMEM((2, ports, rows), F32),
            pltpu.VMEM((ports, rows), F32),
            pltpu.VMEM((ports, rows), F32),
            pltpu.VMEM((ports, ports), F32),
            pltpu.VMEM((h_rows, ports), F32),
            pltpu.VMEM((nr, h_rows, ports), F32),
            pltpu.VMEM((nc, h_rows, ports), F32),
            pltpu.VMEM((ports, ports), F32),
            pltpu.VMEM((8, ports), F32),
            pltpu.VMEM((8, ports), F32),
            pltpu.VMEM((nr, 8, ports), F32),
            pltpu.VMEM((nc, 8, ports), F32),
        ]
        + [sem]
        + gather_sems
        + [sem, sem((nc - 1,)), sem, sem((2 * nz,)), sem, sem((2,))]
        + [sem] * 12,
        compiler_params=pltpu.CompilerParams(
            collective_id=1, has_side_effects=True, vmem_limit_bytes=58 * 2**20
        ),
        name="krylov",
    )(
        slots, got_tiles, right_start, left_start,
        node_diagonal[:, None], node_diagonal[None, :], row_scale[:, None], scale_row,
    )
    return tuple(
        pl.pallas_call(
            finish_kernel,
            out_shape=(
                jax.ShapeDtypeStruct((rows, ports), F32),
                jax.ShapeDtypeStruct((rows, ports), F32),
                jax.ShapeDtypeStruct((ITERS, ports, ports), F32),
            ),
            in_specs=[vmem] * 4,
            out_specs=(vmem,) * 3,
            name="finish",
        )(right_rest, left_rest, norms, projections)
    )


def solution(mesh):
    return jax.shard_map(
        local,
        mesh=mesh,
        in_specs=(
            P(("row", "col"), None, None),
            P(("row", "col")),
            P(("row", "col"), None),
            P(("row", "col"), None),
            P(("row", "col")),
            P(("row", "col")),
        ),
        out_specs=(P(("row", "col"), None), P(("row", "col"), None), P()),
        check_vma=False,
    )
```
